512 devices in a mesh: gz: 16 (over z_lo, x, core), xy: 32 (over z_hi, y).
Axes of the slice: x: 4, y: 8, z: 8 (z_hi: 4, z_lo: 2; z = z_hi * 2 + z_lo), core: 2. Of those that a mesh axis runs over, the one named last changes fastest.
Arguments:
- loaded_planes: bfloat16 [4, 16, 1, 32, 64, 128], P(None, 'gz', None, 'xy'), may hold values from -6 to 6
- first_kernel: bfloat16 [16, 4, 3, 3, 3], replicated, may hold values from -0.625 to 0.625
- first_bias: float32 [16], replicated, may hold values from -3 to 3
- second_kernel: bfloat16 [32, 16, 3, 3, 3], replicated, may hold values from -0.3125 to 0.3125
- second_bias: float32 [32], replicated, may hold values from -3 to 3
- cotangent: bfloat16 [32, 256, 32, 64], P(None, 'gz', 'xy'), may hold values from -6 to 6
Outputs:
- features: bfloat16 [32, 256, 32, 64], P(None, 'gz', 'xy')
- input_grad: bfloat16 [4, 512, 64, 128], P(None, 'gz', 'xy')
- first_kernel_grad: float32 [16, 4, 3, 3, 3], replicated
- first_bias_grad: float32 [16], replicated
- second_kernel_grad: float32 [32, 16, 3, 3, 3], replicated
- second_bias_grad: float32 [32], replicated
The draws below stay inside these ranges and needn't reach their ends.
All inputs are finite; a program needn't handle non-finite values.
Results may differ from the reference program's by a relative error of at most 0.009.
Values may be sent and summed in bfloat16 or wider, within the bound.
No kernel may reach another device: no remote copies, remote signals or barrier semaphores. Data moves between devices by JAX's collectives and lax.ppermute only.
A program may use at most 128 MiB of HBM per device.

```python
import jax
import jax.numpy as jnp
from jax import lax

C_IN = 4
CH1 = 16
CH2 = 32
PLANES_DEV = 1
NY = 128
CZ = 32
NZ = 512
NX = 64
N_GZ = 16
N_XY = 32


def block_levels(rng, shape, shards, low, high):
    loudness = 1.0
    for dim, blocks in shards:
        draws = jax.random.uniform(jax.random.fold_in(jax.random.fold_in(rng, 6), dim), (blocks,), jnp.float32, low / len(shards), high / len(shards))
        loudness = loudness * jnp.repeat(jnp.exp(draws), shape[dim] // blocks).reshape((-1,) + (1,) * (len(shape) - 1 - dim))
    return loudness


def centred(own_key, extent, scale, limit, cuts=(), kind=jnp.bfloat16):
    level = block_levels(own_key, extent, cuts, -0.22, 0.18) if cuts else 1.0
    values = jax.random.normal(own_key, extent, jnp.float32) * scale * level
    return jnp.minimum(jnp.maximum(values, -limit), limit).astype(kind)


def setup_inputs(seed: int = 0) -> dict:
    key_of = jax.random.split(jax.random.key(seed), 7)
    loaded_planes = centred(key_of[0], (C_IN, N_GZ, PLANES_DEV, N_XY, NX, NY), 1.0, 6.0, ((1, 16), (3, 32)))
    first_kernel = centred(key_of[1], (CH1, C_IN, 3, 3, 3), (27 * C_IN) ** -0.5, 0.625)
    first_bias = centred(key_of[2], (CH1,), 0.5, 3.0, (), jnp.float32)
    second_kernel = centred(key_of[3], (CH2, CH1, 3, 3, 3), (27 * CH1) ** -0.5, 0.3125)
    second_bias = centred(key_of[4], (CH2,), 0.5, 3.0, (), jnp.float32)
    cotangent = centred(key_of[5], (CH2, NZ // 2, NX // 2, NY // 2), 1.0, 6.0, ((1, 16), (2, 32)))
    return {"loaded_planes": loaded_planes, "first_kernel": first_kernel, "first_bias": first_bias, "second_kernel": second_kernel, "second_bias": second_bias, "cotangent": cotangent}


NUMS = ('NCDHW', 'OIDHW', 'NCDHW')
HIGH = lax.Precision.HIGHEST

def conv_first(tensor, kernel):
    return lax.conv_general_dilated(tensor[None].astype(jnp.float32), kernel.astype(jnp.float32), (1, 1, 1), ((0, 0), (0, 0), (1, 1)), dimension_numbers=NUMS, precision=HIGH)[0]

def conv_second(tensor, kernel):
    return lax.conv_general_dilated(tensor[None].astype(jnp.float32), kernel.astype(jnp.float32), (2, 2, 2), ((0, 0), (0, 0), (1, 0)), dimension_numbers=NUMS, precision=HIGH)[0]

def back_first(tensor, kernel):
    flipped = kernel.astype(jnp.float32)[:, :, ::-1, ::-1, ::-1].transpose(1, 0, 2, 3, 4)
    return lax.conv_general_dilated(tensor[None].astype(jnp.float32), flipped, (1, 1, 1), ((0, 0), (0, 0), (1, 1)), dimension_numbers=NUMS, precision=HIGH)[0]

def back_second(grads, kernel, shape):
    dummy = jnp.zeros(shape, jnp.float32)
    _, pullback = jax.vjp(lambda values: conv_second(values, kernel), dummy)
    return pullback(grads.astype(jnp.float32))[0]

def kernel_first(source, grads):
    padded = jnp.pad(source.astype(jnp.float32), ((0, 0), (0, 0), (0, 0), (1, 1)))
    depth_z, depth_x, depth_y = (grads.shape[1], grads.shape[2], grads.shape[3])
    flat_grads = grads.astype(jnp.float32).reshape(grads.shape[0], -1)
    blocks = []
    for shift_z in range(3):
        for shift_x in range(3):
            for shift_y in range(3):
                patch_rows = padded[:, shift_z:shift_z + depth_z, shift_x:shift_x + depth_x, shift_y:shift_y + depth_y].reshape(source.shape[0], -1)
                blocks.append(jnp.dot(flat_grads, patch_rows.T, precision=HIGH))
    return jnp.stack(blocks, -1).reshape(grads.shape[0], source.shape[0], 3, 3, 3)

def kernel_second(source, grads):
    padded = jnp.pad(source.astype(jnp.float32), ((0, 0), (0, 0), (0, 0), (1, 0)))
    depth_z, depth_x, depth_y = (grads.shape[1], grads.shape[2], grads.shape[3])
    flat_grads = grads.astype(jnp.float32).reshape(grads.shape[0], -1)
    blocks = []
    for shift_z in range(3):
        for shift_x in range(3):
            for shift_y in range(3):
                patch_rows = padded[:, shift_z:shift_z + 2 * depth_z:2, shift_x:shift_x + 2 * depth_x:2, shift_y:shift_y + 2 * depth_y:2].reshape(source.shape[0], -1)
                blocks.append(jnp.dot(flat_grads, patch_rows.T, precision=HIGH))
    return jnp.stack(blocks, -1).reshape(grads.shape[0], source.shape[0], 3, 3, 3)

def silu_slope(values):
    sigma = jax.nn.sigmoid(values)
    return sigma * (1.0 + values * (1.0 - sigma))

def reference(loaded_planes, first_kernel, first_bias, second_kernel, second_bias, cotangent):
    volume = loaded_planes.reshape(C_IN, NZ, NX, NY)
    padded = jnp.pad(volume, ((0, 0), (2, 2), (1, 1), (0, 0)))
    grad_pad = jnp.pad(cotangent, ((0, 0), (1, 1), (0, 0), (0, 0)))
    half_depth = CZ // 2

    def slab(totals, slab_index):
        first_plane = (slab_index * CZ).astype(jnp.int32)
        window = lax.dynamic_slice_in_dim(padded, first_plane, CZ + 4, 1)
        preact = conv_first(window, first_kernel) + first_bias[:, None, None, None]
        depth = first_plane - 1 + jnp.arange(CZ + 2, dtype=jnp.int32)
        inside = ((depth >= 0) & (depth < NZ)).astype(jnp.float32)[None, :, None, None]
        hidden = (jax.nn.silu(preact) * inside).astype(jnp.bfloat16)
        framed = jnp.pad(hidden[:, :CZ + 1], ((0, 0), (0, 0), (1, 0), (0, 0)))
        features = (conv_second(framed, second_kernel) + second_bias[:, None, None, None]).astype(jnp.bfloat16)
        grad_window = lax.dynamic_slice_in_dim(grad_pad, (slab_index * half_depth).astype(jnp.int32), half_depth + 2, 1)
        raw_grad = back_second(grad_window, second_kernel, (CH1, CZ + 5, NX + 1, NY))[:, 2:CZ + 4, 1:]
        hidden_grad = (raw_grad * silu_slope(preact) * inside).astype(jnp.bfloat16)
        rimmed = jnp.pad(hidden_grad, ((0, 0), (0, 0), (1, 1), (0, 0)))
        input_grad = back_first(rimmed, first_kernel).astype(jnp.bfloat16)
        own_grad = grad_window[:, 1:half_depth + 1]
        own_hidden = hidden_grad[:, 1:CZ + 1]
        first_term = kernel_first(window[:, 1:CZ + 3], own_hidden)
        first_bias_term = lax.optimization_barrier(jnp.sum(own_hidden.astype(jnp.float32), axis=(1, 2, 3)))
        second_term = kernel_second(framed, own_grad)
        second_bias_term = lax.optimization_barrier(jnp.sum(own_grad.astype(jnp.float32), axis=(1, 2, 3)))
        totals = (totals[0] + first_term, totals[1] + first_bias_term, totals[2] + second_term, totals[3] + second_bias_term)
        return (totals, (features, input_grad))
    start_sums = (jnp.zeros((CH1, C_IN, 3, 3, 3), jnp.float32), jnp.zeros((CH1,), jnp.float32), jnp.zeros((CH2, CH1, 3, 3, 3), jnp.float32), jnp.zeros((CH2,), jnp.float32))
    totals, stacked = lax.scan(slab, start_sums, jnp.arange(N_GZ, dtype=jnp.int32))
    features = stacked[0].transpose(1, 0, 2, 3, 4).reshape(CH2, NZ // 2, NX // 2, NY // 2)
    input_grad = stacked[1].transpose(1, 0, 2, 3, 4).reshape(C_IN, NZ, NX, NY)
    grad_scale = 1.0 / (float(NZ) * float(NX) * float(NY)) ** 0.5
    return (features, input_grad, totals[0] * grad_scale, totals[1] * grad_scale, totals[2] * grad_scale, totals[3] * grad_scale)
```

```python
import functools
import math

import jax
import jax.numpy as jnp
import numpy as np
from jax import lax
from jax.experimental import pallas as pl
from jax.experimental.pallas import tpu as pltpu
from jax.sharding import PartitionSpec as P

BF16 = jnp.bfloat16
F32 = jnp.float32
WINDOW = 8
COLUMNS = 4
VMEM_LIMIT = 48 * 1024 * 1024


def shifted(value, axis, steps):
    count = lax.axis_size(axis)
    first, last = (max(0, -steps), min(count, count - steps))
    return lax.ppermute(value, axis, [(source, source + steps) for source in range(first, last)])


def mm(left, right):
    return jnp.dot(left, right, preferred_element_type=F32)


def mm_nt(left, right):
    return lax.dot_general(left, right, (((1,), (1,)), ((), ())), preferred_element_type=F32)


def from_left(value):
    lane = lax.broadcasted_iota(jnp.int32, value.shape, 1)
    return jnp.where(lane == 0, 0.0, pltpu.roll(value, 1, 1))


def from_right(value):
    lane = lax.broadcasted_iota(jnp.int32, value.shape, 1)
    last = value.shape[1] - 1
    return jnp.where(lane == last, 0.0, pltpu.roll(value, last, 1))


def pack_kernel(planes_ref, out_ref, wide_ref):
    channels, width, _ = planes_ref.shape
    wide_ref[...] = jnp.zeros_like(wide_ref)
    wide_ref[:, 8 : 8 + width, :] = planes_ref[...].astype(F32)
    targets = out_ref.shape[0]
    row = lax.broadcasted_iota(jnp.int32, (WINDOW, out_ref.shape[2]), 0)
    for t in range(targets):
        parts = [wide_ref[i, 6 + 2 * t : 6 + 2 * t + WINDOW, :] for i in range(channels)]
        parts = [jnp.where(row >= WINDOW - 2, 1.0, part) for part in parts]
        out_ref[t] = jnp.concatenate(parts, axis=0).astype(BF16)


def pack(planes, targets):
    channels, width, depth_y = planes.shape
    shape = (targets, channels * WINDOW, depth_y)
    return pl.pallas_call(
        pack_kernel,
        out_shape=jax.ShapeDtypeStruct(shape, BF16),
        scratch_shapes=[pltpu.VMEM((channels, width + 16, depth_y), F32)],
        compiler_params=pltpu.CompilerParams(vmem_limit_bytes=VMEM_LIMIT),
        name="pack_windows",
    )(planes)


def prep_kernel(left_ref, mid_ref, right_ref, odd_ref, even_ref, raw_ref, shifts_ref, wide_ref):
    levels, ch2, half_y = mid_ref.shape
    rows = 3 * ch2
    depth_y = 2 * half_y
    spread = (
        2 * lax.broadcasted_iota(jnp.int32, (half_y, depth_y), 0)
        == lax.broadcasted_iota(jnp.int32, (half_y, depth_y), 1)
    ).astype(F32).astype(BF16)
    for q in range(levels):
        block = jnp.concatenate([left_ref[q], mid_ref[q], right_ref[q]], axis=0)
        wide = mm(block, spread)
        wide_ref[pl.ds(q * rows, rows), :] = wide.astype(BF16)
        if 0 < q < levels - 1:
            own = wide[ch2 : 2 * ch2]
            base = (q - 1) * rows
            shifts_ref[pl.ds(base, ch2), :] = from_right(own).astype(BF16)
            shifts_ref[pl.ds(base + ch2, ch2), :] = own.astype(BF16)
            shifts_ref[pl.ds(base + 2 * ch2, ch2), :] = from_left(own).astype(BF16)
    size = raw_ref.shape[0] // (2 * (levels - 1))

    def combine(terms):
        return from_right(terms[:size]) + terms[size : 2 * size] + from_left(terms[2 * size :])

    def level(m, _):
        base = pl.multiple_of(m * rows, rows)
        odd = mm(odd_ref[...], wide_ref[pl.ds(base, 2 * rows), :])
        out = pl.multiple_of(m * 2 * size, 2 * size)
        raw_ref[pl.ds(out, size), :] = combine(odd)
        even = mm(even_ref[...], wide_ref[pl.ds(base + rows, rows), :])
        raw_ref[pl.ds(out + size, size), :] = combine(even)
        return 0

    lax.fori_loop(0, levels - 1, level, 0)


def prep(left, mid, right, odd, even, ch1):
    levels, ch2, half_y = mid.shape
    depth_y = 2 * half_y
    return pl.pallas_call(
        prep_kernel,
        out_shape=(
            jax.ShapeDtypeStruct((2 * (levels - 1) * COLUMNS * ch1, depth_y), F32),
            jax.ShapeDtypeStruct(((levels - 2) * 3 * ch2, depth_y), BF16),
        ),
        scratch_shapes=[pltpu.VMEM((levels * 3 * ch2, depth_y), BF16)],
        compiler_params=pltpu.CompilerParams(vmem_limit_bytes=VMEM_LIMIT),
        name="spread_cotangent",
    )(left, mid, right, odd, even)


def main_kernel(
    place_ref,
    low_ref,
    mid_ref,
    high_ref,
    raw_ref,
    shifts_ref,
    w1_ref,
    b1_ref,
    hidden_ref,
    grad_ref,
    sums_ref,
    vol_ref,
    *,
    ch1,
    ch2,
):
    depth_z, rows, depth_y = mid_ref.shape
    size = COLUMNS * ch1
    vol_ref[pl.ds(0, 2 * rows), :] = low_ref[...].reshape(2 * rows, depth_y)
    vol_ref[pl.ds(2 * rows, depth_z * rows), :] = mid_ref[...].reshape(depth_z * rows, depth_y)
    vol_ref[pl.ds((depth_z + 2) * rows, 2 * rows), :] = high_ref[...].reshape(2 * rows, depth_y)
    at_first_z, at_last_z, at_first_x, at_last_x = (place_ref[k] for k in range(4))
    row = lax.broadcasted_iota(jnp.int32, (size, depth_y), 0)
    outside = ((row < ch1) & (at_first_x != 0)) | ((row >= 3 * ch1) & (at_last_x != 0))
    bias = jnp.broadcast_to(b1_ref[...], (size, depth_y))

    def level(z, _):
        base = pl.multiple_of(z * rows, rows)
        terms = mm(w1_ref[...], vol_ref[pl.ds(base, 3 * rows), :])
        pre = from_left(terms[:size]) + terms[size : 2 * size] + from_right(terms[2 * size :]) + bias
        sigma = 1.0 / (1.0 + jnp.exp(-pre))
        gone = ((z == 0) & (at_first_z != 0)) | ((z == depth_z + 1) & (at_last_z != 0))
        drop = outside | gone
        hidden = jnp.where(drop, 0.0, pre * sigma)
        out = pl.multiple_of(z * size, size)
        raw = raw_ref[pl.ds(out, size), :]
        grad = jnp.where(drop, 0.0, raw * (sigma * (1.0 + pre * (1.0 - sigma))))
        hidden_ref[pl.ds(out, size), :] = jnp.where(row >= 3 * ch1, 1.0, hidden).astype(BF16)
        grad_ref[pl.ds(out, size), :] = grad.astype(BF16)
        return 0

    lax.fori_loop(0, depth_z + 2, level, 0)

    def first(z, total):
        out = pl.multiple_of((z + 1) * size, size)
        own = grad_ref[pl.ds(out + ch1, 2 * ch1), :].astype(F32)
        parts = [from_right(own), own, from_left(own)]
        sides = [part[x * ch1 : (x + 1) * ch1] for x in range(2) for part in parts]
        moved = jnp.concatenate(sides, axis=0).astype(BF16)
        base = pl.multiple_of((z + 1) * rows, rows)
        return total + mm_nt(vol_ref[pl.ds(base, 3 * rows), :], moved)

    first_sum = lax.fori_loop(0, depth_z, first, jnp.zeros((3 * rows, 6 * ch1), F32))

    def second(q, total):
        base = pl.multiple_of(q * 2 * size, 2 * size)
        own = pl.multiple_of(q * 3 * ch2, 3 * ch2)
        return total + mm_nt(hidden_ref[pl.ds(base, 3 * size), :], shifts_ref[pl.ds(own, 3 * ch2), :])

    second_sum = lax.fori_loop(0, depth_z // 2, second, jnp.zeros((3 * size, 3 * ch2), F32))
    folded = first_sum[:, : 3 * ch1] + pltpu.roll(first_sum, 3 * rows - 1, 0)[:, 3 * ch1 :]
    sums_ref[:, : 3 * ch2] = second_sum
    sums_ref[: 3 * rows, 3 * ch2 : 3 * ch2 + ch1] = folded[:, :ch1]
    sums_ref[: 3 * rows, 3 * ch2 + ch1 :] = folded[:, ch1 : 2 * ch1]
    sums_ref[3 * rows :, 3 * ch2 : 3 * ch2 + ch1] = folded[:, 2 * ch1 :]
    sums_ref[3 * rows :, 3 * ch2 + ch1 :] = jnp.zeros((3 * size - 3 * rows, ch1), F32)


def main(place, low, mid, high, raw, shifts, w1, b1, ch1, ch2):
    depth_z, rows, depth_y = mid.shape
    size = COLUMNS * ch1
    vmem = pl.BlockSpec(memory_space=pltpu.VMEM)
    return pl.pallas_call(
        functools.partial(main_kernel, ch1=ch1, ch2=ch2),
        in_specs=[pl.BlockSpec(memory_space=pltpu.SMEM)] + [vmem] * 7,
        out_specs=(vmem, vmem, vmem),
        out_shape=(
            jax.ShapeDtypeStruct(((depth_z + 2) * size, depth_y), BF16),
            jax.ShapeDtypeStruct(((depth_z + 2) * size, depth_y), BF16),
            jax.ShapeDtypeStruct((3 * size, 128), F32),
        ),
        scratch_shapes=[pltpu.VMEM(((depth_z + 4) * rows, depth_y), BF16)],
        compiler_params=pltpu.CompilerParams(vmem_limit_bytes=VMEM_LIMIT),
        name="hidden_and_sums",
    )(place, low, mid, high, raw, shifts, w1, b1)


def last_kernel(hidden_ref, grad_ref, w2_ref, b2_ref, w4_ref, feat_ref, gin_ref, featw_ref, ginw_ref):
    ch2, depth_q, half_y = feat_ref.shape
    c_in, _, depth_y = gin_ref.shape
    size = hidden_ref.shape[0] // (2 * depth_q + 2)
    bias = jnp.broadcast_to(b2_ref[...], (ch2, depth_y))
    pick = (
        lax.broadcasted_iota(jnp.int32, (depth_y, half_y), 0)
        == 2 * lax.broadcasted_iota(jnp.int32, (depth_y, half_y), 1)
    ).astype(F32).astype(BF16)

    for q in range(depth_q):
        base = q * 2 * size
        terms = mm(w2_ref[...], hidden_ref[pl.ds(base, 3 * size), :])
        full = from_left(terms[:ch2]) + terms[ch2 : 2 * ch2] + from_right(terms[2 * ch2 :]) + bias
        featw_ref[pl.ds(q, ch2, stride=depth_q), :] = mm(full.astype(BF16), pick)
    feat_ref[...] = featw_ref[...].reshape(feat_ref.shape).astype(BF16)

    two = 2 * c_in
    for z in range(2 * depth_q):
        base = z * size
        terms = mm(w4_ref[...], grad_ref[pl.ds(base, 3 * size), :])
        full = from_right(terms[:two]) + terms[two : 2 * two] + from_left(terms[2 * two :])
        for x in range(2):
            ginw_ref[pl.ds(2 * z + x, c_in, stride=4 * depth_q), :] = full[x * c_in : (x + 1) * c_in]
    gin_ref[...] = ginw_ref[...].reshape(gin_ref.shape).astype(BF16)


def last(hidden, grad, w2, b2, w4, c_in, ch2):
    depth_y = hidden.shape[1]
    ch1 = w2.shape[1] // (3 * COLUMNS)
    depth_z = hidden.shape[0] // (COLUMNS * ch1) - 2
    depth_q = depth_z // 2
    return pl.pallas_call(
        last_kernel,
        out_shape=(
            jax.ShapeDtypeStruct((ch2, depth_q, depth_y // 2), BF16),
            jax.ShapeDtypeStruct((c_in, 2 * depth_z, depth_y), BF16),
        ),
        scratch_shapes=[
            pltpu.VMEM((ch2 * depth_q, depth_y // 2), F32),
            pltpu.VMEM((c_in * 2 * depth_z, depth_y), F32),
        ],
        compiler_params=pltpu.CompilerParams(vmem_limit_bytes=VMEM_LIMIT),
        name="features_and_input_grad",
    )(hidden, grad, w2, b2, w4)


def unpack_kernel(sums_ref, first_ref, second_ref, bias1_ref, bias2_ref, *, scale):
    _, c_in, ch1 = first_ref.shape
    ch2 = second_ref.shape[2]
    rows = 3 * c_in * WINDOW
    size = COLUMNS * ch1
    at = 3 * ch2
    corners = ((0, at), (0, at + ch1), (rows, at))
    for a in range(3):
        for b in range(3):
            for c in range(3):
                k = 9 * a + 3 * b + c
                block = sums_ref[a * size + b * ch1 : a * size + (b + 1) * ch1, c * ch2 : (c + 1) * ch2]
                second_ref[k] = block * scale
                down, right = corners[c]
                base = down + a * c_in * WINDOW + b + 1
                block = sums_ref[pl.ds(base, c_in, stride=WINDOW), :]
                first_ref[k] = block[:, right : right + ch1] * scale
    bias2_ref[...] = sums_ref[size + 3 * ch1 : size + 3 * ch1 + 1, ch2 : 2 * ch2] * scale
    down, right = corners[1]
    base = down + c_in * WINDOW + WINDOW - 2
    bias1_ref[...] = sums_ref[base : base + 1, right : right + ch1] * scale


def unpack(sums, scale, c_in, ch1, ch2):
    first, bias1, second, bias2 = (
        jax.ShapeDtypeStruct(shape, F32) for shape in ((27, c_in, ch1), (1, ch1), (27, ch1, ch2), (1, ch2))
    )
    first, second, bias1, bias2 = pl.pallas_call(
        functools.partial(unpack_kernel, scale=scale),
        out_shape=(first, second, bias1, bias2),
        name="unpack_sums",
    )(sums)
    first = first.reshape(3, 3, 3, c_in, ch1).transpose(4, 3, 0, 1, 2)
    second = second.reshape(3, 3, 3, ch1, ch2).transpose(4, 3, 0, 1, 2)
    return first, bias1[0], second, bias2[0]


def total_over_devices(sums):
    slabs, tiles = lax.axis_size("gz"), lax.axis_size("xy")
    near, row = slabs // 2, tiles // 4
    far, cols = slabs // near, tiles // row
    both = ("gz", "xy")
    near_groups = [[f * near + k for k in range(near)] for f in range(far)]
    far_groups = [
        [(f * near + k) * tiles + c * row + r for c in range(cols) for f in range(far)]
        for k in range(near)
        for r in range(row)
    ]
    row_groups = [[c * row + r for r in range(row)] for c in range(cols)]

    def exchange(value, axis, groups):
        return lax.all_to_all(value, axis, 0, 0, tiled=True, axis_index_groups=groups)

    def spread(value, axis, groups):
        count = len(groups[0])
        return exchange(jnp.broadcast_to(value[None], (count,) + value.shape), axis, groups)

    part = exchange(sums.reshape(near, -1, sums.shape[1]), "gz", near_groups).sum(0)
    part = spread(part, both, far_groups).sum(0)
    part = spread(part, "xy", row_groups).sum(0)
    return spread(part, "gz", near_groups).reshape(sums.shape)


def one_hot(shape, test):
    return jnp.asarray(np.fromfunction(np.vectorize(test), shape, dtype=int).astype(np.float32)).astype(BF16)


def weight_matrices(first_kernel, second_kernel):
    ch1, c_in = first_kernel.shape[:2]
    ch2 = second_kernel.shape[0]
    size = COLUMNS * ch1
    to_window = one_hot((COLUMNS, 3, WINDOW), lambda x, b, w: w == x + b)
    w1 = jnp.einsum("oiabc,xbw->cxoaiw", first_kernel, to_window, preferred_element_type=BF16)
    w1 = w1.reshape(3 * size, 3 * c_in * WINDOW)
    padded = jnp.pad(second_kernel, ((0, 0), (0, 0), (0, 0), (0, COLUMNS - 3), (0, 0)))
    w2 = padded.transpose(4, 0, 2, 3, 1).reshape(3 * ch2, 3 * size)
    from_cot = one_hot((COLUMNS, 3, 3), lambda x, q, b: x - 1 == 2 * (q - 1) + b - 1)
    w3 = jnp.einsum("oiabc,xqb->acxiqo", second_kernel, from_cot, preferred_element_type=BF16)
    w3 = w3.reshape(3, 3 * size, 3 * ch2)
    odd = jnp.concatenate([w3[2], w3[0]], axis=1)
    own = one_hot((2, COLUMNS, 3), lambda x, w, b: w == x + 2 - b)
    w4 = jnp.einsum("oiabc,xwb->cxiawo", first_kernel[:, :, ::-1], own, preferred_element_type=BF16)
    w4 = w4.reshape(3 * 2 * c_in, 3 * size)
    return w1, w2, odd, w3[1], w4


def shards(loaded_planes, first_kernel, first_bias, second_kernel, second_bias, cotangent):
    channels, _, planes_dev, _, width, depth_y = loaded_planes.shape
    tiles = lax.axis_size("xy")
    slabs = lax.axis_size("gz")
    ch1, ch2 = first_kernel.shape[0], second_kernel.shape[0]
    depth_z = planes_dev * tiles

    windows = pack(loaded_planes.reshape(channels, width, depth_y), tiles)
    mid = lax.all_to_all(windows, "xy", split_axis=0, concat_axis=0, tiled=True)

    cot = cotangent[:, :, 0].transpose(1, 0, 2)
    cot = jnp.concatenate([shifted(cot[-1:], "gz", 1), cot, shifted(cot[:1], "gz", -1)], axis=0)
    left, right = shifted(cot, "xy", 1), shifted(cot, "xy", -1)
    w1, w2, odd, even, w4 = weight_matrices(first_kernel, second_kernel)
    raw, shifts = prep(left, cot, right, odd, even, ch1)

    low, high = shifted(mid[-2:], "gz", 1), shifted(mid[:2], "gz", -1)
    g, t = lax.axis_index("gz"), lax.axis_index("xy")
    place = jnp.stack([g == 0, g == slabs - 1, t == 0, t == tiles - 1]).astype(jnp.int32)
    b1 = jnp.tile(first_bias, COLUMNS)[:, None]
    hidden, grad, sums = main(place, low, mid, high, raw, shifts, w1, b1, ch1, ch2)
    sums = total_over_devices(sums)
    features, input_grad = last(hidden, grad, w2, second_bias[:, None], w4, channels, ch2)
    scale = 1.0 / math.sqrt(slabs * depth_z * width * depth_y)
    first_grad, first_bias_grad, second_grad, second_bias_grad = unpack(sums, scale, channels, ch1, ch2)
    return (
        features[:, :, None, :],
        input_grad.reshape(channels, depth_z, 2, depth_y),
        first_grad,
        first_bias_grad,
        second_grad,
        second_bias_grad,
    )


def solution(mesh):
    return jax.shard_map(
        shards,
        mesh=mesh,
        in_specs=(
            P(None, "gz", None, "xy", None, None),
            P(),
            P(),
            P(),
            P(),
            P(None, "gz", "xy", None),
        ),
        out_specs=(P(None, "gz", "xy", None), P(None, "gz", "xy", None), P(), P(), P(), P()),
        check_vma=False,
    )
```

```python
import functools
import math

import jax
import jax.numpy as jnp
from jax import lax
from jax.experimental import pallas as pl
from jax.experimental.pallas import tpu as pltpu
from jax.sharding import PartitionSpec as P

BF16 = jnp.bfloat16
F32 = jnp.float32
WINDOW = 8
COLUMNS = 4
VMEM_LIMIT = 48 * 1024 * 1024


def shifted(value, axis, steps):
    count = lax.axis_size(axis)
    first, last = (max(0, -steps), min(count, count - steps))
    return lax.ppermute(value, axis, [(source, source + steps) for source in range(first, last)])


def mm(left, right):
    return jnp.dot(left, right, preferred_element_type=F32)


def mm_nt(left, right):
    return lax.dot_general(left, right, (((1,), (1,)), ((), ())), preferred_element_type=F32)


def from_left(value):
    lane = lax.broadcasted_iota(jnp.int32, value.shape, 1)
    return jnp.where(lane == 0, 0.0, pltpu.roll(value, 1, 1))


def from_right(value):
    lane = lax.broadcasted_iota(jnp.int32, value.shape, 1)
    last = value.shape[1] - 1
    return jnp.where(lane == last, 0.0, pltpu.roll(value, last, 1))


def lanes(blocks):
    return blocks[0] if len(blocks) == 1 else jnp.concatenate(blocks, axis=1)


def pack_kernel(planes_ref, out_ref, wide_ref):
    channels, width, _ = planes_ref.shape
    wide_ref[...] = jnp.zeros_like(wide_ref)
    wide_ref[:, 8 : 8 + width, :] = planes_ref[...].astype(F32)
    targets = out_ref.shape[0]
    row = lax.broadcasted_iota(jnp.int32, (WINDOW, out_ref.shape[2]), 0)
    for t in range(targets):
        parts = [wide_ref[i, 6 + 2 * t : 6 + 2 * t + WINDOW, :] for i in range(channels)]
        parts = [jnp.where(row >= WINDOW - 2, 1.0, part) for part in parts]
        out_ref[t] = jnp.concatenate(parts, axis=0).astype(BF16)


def pack(planes, targets):
    channels, width, depth_y = planes.shape
    shape = (targets, channels * WINDOW, depth_y)
    return pl.pallas_call(
        pack_kernel,
        out_shape=jax.ShapeDtypeStruct(shape, BF16),
        scratch_shapes=[pltpu.VMEM((channels, width + 16, depth_y), F32)],
        compiler_params=pltpu.CompilerParams(vmem_limit_bytes=VMEM_LIMIT),
        name="pack_windows",
    )(planes)


def split_bias(bias):
    high = bias.astype(BF16).astype(F32)
    middle = (bias - high).astype(BF16).astype(F32)
    return high, middle, bias - high - middle


def first_matrix(kernel_ref, bias_ref, turned_ref):
    _, c_in, ch1 = kernel_ref.shape
    size = COLUMNS * ch1
    turned_ref[...] = jnp.zeros_like(turned_ref)
    nothing = jnp.zeros((c_in, ch1), F32)

    def block(a, b, c):
        return kernel_ref[9 * a + 3 * b + c].astype(F32) if 0 <= b < 3 and c < 3 else nothing

    for a in range(3):
        for w in range(COLUMNS + 2):
            at = pl.ds(a * c_in * WINDOW + w, c_in, stride=WINDOW)
            for half in range(2):
                blocks = [block(a, w - x, c) for c in (2 * half, 2 * half + 1) for x in range(COLUMNS)]
                turned_ref[half, at, :] = jnp.concatenate(blocks, axis=1)
    for n, part in enumerate(split_bias(bias_ref[...])):
        row = c_in * WINDOW + n * WINDOW + WINDOW - 2
        for x in range(COLUMNS):
            half, right = divmod(size + x * ch1, 128)
            turned_ref[half, row : row + 1, right : right + ch1] = part
    return jnp.concatenate([turned_ref[0].T, turned_ref[1].T], axis=0)[: 3 * size].astype(BF16)


def spread_matrix(kernel_ref, out_ref, row, a, column):
    _, ch1, ch2 = kernel_ref.shape
    for c in range(3):
        for x in range(COLUMNS):
            for q in range(3):
                b = x - 1 - 2 * (q - 1) + 1
                if 0 <= b <= 2:
                    down, right = row + (c * COLUMNS + x) * ch1, column + q * ch2
                    out_ref[down : down + ch1, right : right + ch2] = kernel_ref[9 * a + 3 * b + c]


def unspread(terms):
    size = terms.shape[0] // 3
    return from_right(terms[:size]) + terms[size : 2 * size] + from_left(terms[2 * size :])


def prep_kernel(
    left_ref,
    mid_ref,
    right_ref,
    k1_ref,
    b1_ref,
    k2_ref,
    raw_ref,
    shifts_ref,
    ends_ref,
    w1_ref,
    odd_ref,
    even_ref,
    wide_ref,
    flat_ref,
    turned_ref,
):
    ch2, cells, half_y = mid_ref.shape
    rows = 3 * ch2
    depth_y = 2 * half_y
    w1_ref[...] = first_matrix(k1_ref, b1_ref, turned_ref)
    odd_ref[...] = jnp.zeros_like(odd_ref)
    even_ref[...] = jnp.zeros_like(even_ref)
    spread_matrix(k2_ref, odd_ref, 0, 2, 0)
    spread_matrix(k2_ref, odd_ref, 0, 0, rows)
    spread_matrix(k2_ref, even_ref, 0, 1, 0)
    spread = (
        2 * lax.broadcasted_iota(jnp.int32, (half_y, depth_y), 0)
        == lax.broadcasted_iota(jnp.int32, (half_y, depth_y), 1)
    ).astype(F32).astype(BF16)
    for n, ref in enumerate((left_ref, mid_ref, right_ref)):
        flat_ref[n * ch2 * cells : (n + 1) * ch2 * cells, :] = ref[...].astype(F32).reshape(ch2 * cells, half_y)
    for q in range(cells):
        block = jnp.concatenate(
            [flat_ref[pl.ds(n * ch2 * cells + q, ch2, stride=cells), :] for n in range(3)], axis=0
        )
        wide = mm(block.astype(BF16), spread)
        wide_ref[q * rows : (q + 1) * rows, :] = wide.astype(BF16)
        own = wide[ch2 : 2 * ch2]
        base = q * rows
        shifts_ref[base : base + ch2, :] = from_right(own).astype(BF16)
        shifts_ref[base + ch2 : base + 2 * ch2, :] = own.astype(BF16)
        shifts_ref[base + 2 * ch2 : base + 3 * ch2, :] = from_left(own).astype(BF16)
    ends_ref[:rows, :] = wide_ref[:rows, :]
    ends_ref[rows:, :] = wide_ref[(cells - 1) * rows :, :]
    size = even_ref.shape[0] // 3

    def store(z, terms):
        raw_ref[(z - 1) * size : z * size, :] = unspread(terms)

    for m in range(0, cells - 1, 2):
        group = [k for k in (m, m + 1) if k < cells - 1]
        odd = mm(odd_ref[...], lanes([wide_ref[k * rows : (k + 2) * rows, :] for k in group]))
        even = mm(even_ref[...], lanes([wide_ref[(k + 1) * rows : (k + 2) * rows, :] for k in group]))
        for n, k in enumerate(group):
            store(2 * k + 1, odd[:, n * depth_y : (n + 1) * depth_y])
            store(2 * k + 2, even[:, n * depth_y : (n + 1) * depth_y])


def prep(left, mid, right, k1, b1, k2):
    ch2, cells, half_y = mid.shape
    _, c_in, ch1 = k1.shape
    depth_y = 2 * half_y
    size, rows = COLUMNS * ch1, 3 * ch2
    return pl.pallas_call(
        prep_kernel,
        out_shape=(
            jax.ShapeDtypeStruct((2 * (cells - 1) * size, depth_y), F32),
            jax.ShapeDtypeStruct((cells * rows, depth_y), BF16),
            jax.ShapeDtypeStruct((2 * rows, depth_y), BF16),
            jax.ShapeDtypeStruct((3 * size, 3 * c_in * WINDOW), BF16),
            jax.ShapeDtypeStruct((3 * size, 2 * rows), BF16),
            jax.ShapeDtypeStruct((3 * size, rows), BF16),
        ),
        scratch_shapes=[
            pltpu.VMEM((cells * rows, depth_y), BF16),
            pltpu.VMEM((rows * cells, half_y), F32),
            pltpu.VMEM((2, 3 * c_in * WINDOW, 128), F32),
        ],
        compiler_params=pltpu.CompilerParams(vmem_limit_bytes=VMEM_LIMIT),
        cost_estimate=pl.CostEstimate(flops=800_000_000, bytes_accessed=10_000_000, transcendentals=0),
        name="spread_cotangent",
    )(left, mid, right, k1, b1, k2)


def activate(groups, plane, raw, place_ref, w1_ref, depth_z, store):
    size = w1_ref.shape[0] // 3
    ch1 = size // COLUMNS
    at_first_z, at_last_z, at_first_x, at_last_x = (place_ref[k] for k in range(4))
    depth_y = plane(groups[0][0]).shape[1]
    row = lax.broadcasted_iota(jnp.int32, (size, depth_y), 0)
    outside = ((row < ch1) & (at_first_x != 0)) | ((row >= 3 * ch1) & (at_last_x != 0))
    inside = jnp.where(outside, 0.0, 1.0)
    for group in groups:
        source = lanes([jnp.concatenate([plane(z + a) for a in (-1, 0, 1)], axis=0) for z in group])
        products = mm(w1_ref[...], source)
        for n, z in enumerate(group):
            terms = products[:, n * depth_y : (n + 1) * depth_y]
            pre = from_left(terms[:size]) + terms[size : 2 * size] + from_right(terms[2 * size :])
            sigma = 1.0 / (1.0 + jnp.exp(-pre))
            keep = inside
            if z == -1:
                keep = inside * jnp.where(at_first_z != 0, 0.0, 1.0)
            if z == depth_z:
                keep = inside * jnp.where(at_last_z != 0, 0.0, 1.0)
            kept = sigma * keep
            store(z, (pre * kept)[: 3 * ch1], raw(z) * (kept * (1.0 + pre * (1.0 - sigma))))


def side_by_side(grad, ch1):
    own = grad[ch1 : 3 * ch1]
    parts = [from_right(own), own, from_left(own)]
    sides = [part[x * ch1 : (x + 1) * ch1] for x in range(2) for part in parts]
    return jnp.concatenate(sides, axis=0).astype(BF16)


def add_first(levels, plane, moved, total):
    for k in range(0, len(levels), 2):
        group = levels[k : k + 2]
        source = lanes([jnp.concatenate([plane(z + a) for a in (-1, 0, 1)], axis=0) for z in group])
        product = mm_nt(source, lanes([moved(z) for z in group]))
        total = product if total is None else total + product
    return total


def add_second(cells, hidden, shifts_ref, total_cells, total):
    rows = shifts_ref.shape[0] // total_cells
    for k in range(0, len(cells), 2):
        group = cells[k : k + 2]
        source = lanes([jnp.concatenate([hidden(2 * q + a) for a in (-1, 0, 1)], axis=0) for q in group])
        product = mm_nt(source, lanes([shifts_ref[q * rows : (q + 1) * rows, :] for q in group]))
        total = product if total is None else total + product
    return total


def store_level(hidden_ref, grad_ref, moved_ref, at, hidden, grad, own, ch1):
    size = COLUMNS * ch1
    hidden_ref[at * size : at * size + 3 * ch1, :] = hidden.astype(BF16)
    hidden_ref[at * size + 3 * ch1 : (at + 1) * size, :] = jnp.ones((ch1, hidden.shape[1]), BF16)
    grad_ref[at * size : (at + 1) * size, :] = grad.astype(BF16)
    if own:
        moved_ref[at * 6 * ch1 : (at + 1) * 6 * ch1, :] = side_by_side(grad, ch1)


def inner_kernel(
    place_ref, mid_ref, raw_ref, shifts_ref, w1_ref, hidden_ref, grad_ref, first_ref, second_ref, moved_ref
):
    depth_z = mid_ref.shape[0]
    size = w1_ref.shape[0] // 3
    ch1 = size // COLUMNS
    levels = list(range(1, depth_z - 1))

    def store(z, hidden, grad):
        store_level(hidden_ref, grad_ref, moved_ref, z - 1, hidden, grad, True, ch1)

    def plane(z):
        return mid_ref[z]

    def raw(z):
        return raw_ref[(z - 1) * size : z * size, :]

    groups = [levels[k : k + 2] for k in range(0, len(levels), 2)]
    activate(groups, plane, raw, place_ref, w1_ref, depth_z, store)
    six = 6 * ch1
    first_ref[...] = add_first(levels, plane, lambda z: moved_ref[(z - 1) * six : z * six, :], None)
    cells = list(range(1, depth_z // 2 - 1))

    def hidden(z):
        return hidden_ref[(z - 1) * size : z * size, :]

    second_ref[...] = add_second(cells, hidden, shifts_ref, depth_z // 2, None)


def edge_kernel(
    place_ref,
    low_ref,
    mid_ref,
    high_ref,
    ends_ref,
    odd_ref,
    even_ref,
    shifts_ref,
    w1_ref,
    inner_ref,
    first_ref,
    second_ref,
    hidden_ref,
    grad_ref,
    sums_ref,
    moved_ref,
    fold_ref,
):
    depth_z, rows, depth_y = mid_ref.shape
    size = w1_ref.shape[0] // 3
    ch1 = size // COLUMNS
    ch2 = shifts_ref.shape[0] // (3 * (depth_z // 2))
    places = {-1: 0, 0: 1, depth_z - 1: 2, depth_z: 3}
    spread_rows = 3 * ch2
    below = [low_ref[2 * rows :, :], ends_ref[:spread_rows, :]]
    above = [ends_ref[spread_rows:, :], high_ref[2 * rows :, :]]
    odd = mm(odd_ref[...], lanes([jnp.concatenate(pair, axis=0) for pair in (below, above)]))
    even = mm(even_ref[...], lanes([below[1], above[1]]))
    raws = {
        -1: unspread(odd[:, :depth_y]),
        0: unspread(even[:, :depth_y]),
        depth_z - 1: unspread(odd[:, depth_y:]),
        depth_z: unspread(even[:, depth_y:]),
    }

    def plane(z):
        if z < 0:
            return low_ref[(z + 2) * rows : (z + 3) * rows, :]
        if z >= depth_z:
            return high_ref[(z - depth_z) * rows : (z - depth_z + 1) * rows, :]
        return mid_ref[z]

    def store(z, hidden, grad):
        store_level(hidden_ref, grad_ref, moved_ref, places[z], hidden, grad, 0 <= z < depth_z, ch1)

    groups = [[-1, 0], [depth_z - 1, depth_z]]
    activate(groups, plane, lambda z: raws[z], place_ref, w1_ref, depth_z, store)
    six = 6 * ch1

    def moved(z):
        return moved_ref[places[z] * six : (places[z] + 1) * six, :]

    def hidden(z):
        if z in places:
            return hidden_ref[places[z] * size : (places[z] + 1) * size, :]
        return inner_ref[(z - 1) * size : z * size, :]

    first = add_first([0, depth_z - 1], plane, moved, first_ref[...])
    second = add_second([0, depth_z // 2 - 1], hidden, shifts_ref, depth_z // 2, second_ref[...])
    three = 3 * ch1
    wide = 3 * ch2
    main = 7 * ch1
    for a in range(2):
        sums_ref[a * three : (a + 1) * three, :wide] = second[a * size : a * size + three]
    sums_ref[2 * three : main, :wide] = second[2 * size : 2 * size + ch1]
    rest = second[2 * size + ch1 : 2 * size + three]
    sums_ref[6 * ch1 : main, wide:] = jnp.zeros((ch1, 128 - wide), F32)
    sums_ref[main : main + ch1, :] = jnp.zeros((ch1, 128), F32)
    for c in range(3):
        sums_ref[c * 2 * ch1 : (c + 1) * 2 * ch1, wide:] = rest[:, c * ch2 : (c + 1) * ch2]
    count = first.shape[0]
    fold_ref[...] = first[:, :three] + pltpu.roll(first, count - 1, 0)[:, three:]
    groups = count // WINDOW
    for b in range(3):
        block = fold_ref[pl.ds(b + 1, groups, stride=WINDOW), :]
        if b < 2:
            sums_ref[main : main + groups, b * three : (b + 1) * three] = block
        else:
            sums_ref[main : main + groups, wide : wide + ch1] = block[:, :ch1]
            sums_ref[main : main + groups, wide + ch1 :] = block[:, ch1 : 2 * ch1]
            sums_ref[6 * ch1 : 6 * ch1 + groups, wide : wide + ch1] = block[:, 2 * ch1 :]
    at = count // 3 + WINDOW - 2
    sums_ref[main + groups : main + groups + 1, :ch1] = fold_ref[at : at + 1, ch1 : 2 * ch1]
    at = size + three
    sums_ref[main + groups + 1 : main + groups + 2, :ch2] = second[at : at + 1, ch2 : 2 * ch2]


def inner(place, mid, raw, shifts, w1):
    depth_z, rows, depth_y = mid.shape
    size = w1.shape[0] // 3
    ch1 = size // COLUMNS
    ch2 = shifts.shape[0] // (3 * (depth_z // 2))
    vmem = pl.BlockSpec(memory_space=pltpu.VMEM)
    count = depth_z - 2
    return pl.pallas_call(
        inner_kernel,
        in_specs=[pl.BlockSpec(memory_space=pltpu.SMEM)] + [vmem] * 4,
        out_specs=(vmem,) * 4,
        out_shape=(
            jax.ShapeDtypeStruct((count * size, depth_y), BF16),
            jax.ShapeDtypeStruct((count * size, depth_y), BF16),
            jax.ShapeDtypeStruct((3 * rows, 6 * ch1), F32),
            jax.ShapeDtypeStruct((3 * size, 3 * ch2), F32),
        ),
        scratch_shapes=[pltpu.VMEM((count * 6 * ch1, depth_y), BF16)],
        compiler_params=pltpu.CompilerParams(vmem_limit_bytes=VMEM_LIMIT),
        cost_estimate=pl.CostEstimate(flops=800_000_000, bytes_accessed=10_000_000, transcendentals=500_000),
        name="inner_levels",
    )(place, mid, raw, shifts, w1)


def edge(place, low, mid, high, ends, odd, even, shifts, w1, inner_hidden, first, second):
    _, rows, depth_y = mid.shape
    size = w1.shape[0] // 3
    ch1 = size // COLUMNS
    vmem = pl.BlockSpec(memory_space=pltpu.VMEM)
    return pl.pallas_call(
        edge_kernel,
        in_specs=[pl.BlockSpec(memory_space=pltpu.SMEM)] + [vmem] * 11,
        out_specs=(vmem,) * 3,
        out_shape=(
            jax.ShapeDtypeStruct((4 * size, depth_y), BF16),
            jax.ShapeDtypeStruct((4 * size, depth_y), BF16),
            jax.ShapeDtypeStruct((8 * ch1, 128), F32),
        ),
        scratch_shapes=[pltpu.VMEM((4 * 6 * ch1, depth_y), BF16), pltpu.VMEM((3 * rows, 3 * ch1), F32)],
        compiler_params=pltpu.CompilerParams(vmem_limit_bytes=VMEM_LIMIT),
        name="edge_levels_and_sums",
    )(place, low, mid, high, ends, odd, even, shifts, w1, inner_hidden, first, second)


def last_kernel(
    hidden_ref,
    hidden_edge_ref,
    grad_ref,
    grad_edge_ref,
    k1_ref,
    k2_ref,
    b2_ref,
    feat_ref,
    gin_ref,
    featw_ref,
    ginw_ref,
    turned_ref,
    w4_ref,
):
    ch2, depth_q, half_y = feat_ref.shape
    c_in, _, depth_y = gin_ref.shape
    depth_z = 2 * depth_q
    size = hidden_edge_ref.shape[0] // 4
    places = {-1: 0, 0: 1, depth_z - 1: 2, depth_z: 3}

    def level(inner_ref, edge_ref, z):
        if z in places:
            return edge_ref[places[z] * size : (places[z] + 1) * size, :]
        return inner_ref[(z - 1) * size : z * size, :]

    def window(inner_ref, edge_ref, z):
        return jnp.concatenate([level(inner_ref, edge_ref, z + a) for a in (-1, 0, 1)], axis=0)

    ch1 = size // COLUMNS
    turned_ref[...] = jnp.zeros_like(turned_ref)
    w4_ref[...] = jnp.zeros_like(w4_ref)
    for a in range(3):
        for b in range(3):
            for c in range(3):
                k = 9 * a + 3 * b + c
                down = a * size + b * ch1
                turned_ref[down : down + ch1, c * ch2 : (c + 1) * ch2] = k2_ref[k].astype(F32)
                for x in range(2):
                    down, right = (c * 2 + x) * c_in, (2 - a) * size + (x + 2 - b) * ch1
                    w4_ref[down : down + c_in, right : right + ch1] = k1_ref[k].astype(F32)
    for n, part in enumerate(split_bias(b2_ref[...])):
        row = size + 3 * ch1 + n
        turned_ref[row : row + 1, ch2 : 2 * ch2] = part
    w2 = turned_ref[...].T[: 3 * ch2].astype(BF16)
    w4 = w4_ref[...].astype(BF16)
    pick = (
        lax.broadcasted_iota(jnp.int32, (depth_y, half_y), 0)
        == 2 * lax.broadcasted_iota(jnp.int32, (depth_y, half_y), 1)
    ).astype(F32).astype(BF16)

    for q in range(0, depth_q, 2):
        source = lanes([window(hidden_ref, hidden_edge_ref, 2 * k) for k in (q, q + 1)])
        products = mm(w2, source)
        for n in range(2):
            terms = products[:, n * depth_y : (n + 1) * depth_y]
            full = from_left(terms[:ch2]) + terms[ch2 : 2 * ch2] + from_right(terms[2 * ch2 :])
            featw_ref[pl.ds(q + n, ch2, stride=depth_q), :] = mm(full.astype(BF16), pick)
    feat_ref[...] = featw_ref[...].reshape(feat_ref.shape).astype(BF16)

    two = 2 * c_in
    for z in range(0, depth_z, 2):
        source = lanes([window(grad_ref, grad_edge_ref, k) for k in (z, z + 1)])
        products = mm(w4, source)
        for n in range(2):
            terms = products[:, n * depth_y : (n + 1) * depth_y]
            full = from_right(terms[:two]) + terms[two : 2 * two] + from_left(terms[2 * two :])
            for x in range(2):
                at = pl.ds(2 * (z + n) + x, c_in, stride=2 * depth_z)
                ginw_ref[at, :] = full[x * c_in : (x + 1) * c_in]
    gin_ref[...] = ginw_ref[...].reshape(gin_ref.shape).astype(BF16)


def last(hidden, hidden_edge, grad, grad_edge, k1, k2, b2):
    depth_y = hidden.shape[1]
    size = hidden_edge.shape[0] // 4
    _, c_in, ch1 = k1.shape
    ch2 = k2.shape[2]
    depth_z = hidden.shape[0] // size + 2
    depth_q = depth_z // 2
    return pl.pallas_call(
        last_kernel,
        out_shape=(
            jax.ShapeDtypeStruct((ch2, depth_q, depth_y // 2), BF16),
            jax.ShapeDtypeStruct((c_in, 2 * depth_z, depth_y), BF16),
        ),
        scratch_shapes=[
            pltpu.VMEM((ch2 * depth_q, depth_y // 2), F32),
            pltpu.VMEM((c_in * 2 * depth_z, depth_y), F32),
            pltpu.VMEM((3 * size, 128), F32),
            pltpu.VMEM((3 * 2 * c_in, 3 * size), F32),
        ],
        compiler_params=pltpu.CompilerParams(vmem_limit_bytes=VMEM_LIMIT),
        cost_estimate=pl.CostEstimate(flops=800_000_000, bytes_accessed=10_000_000, transcendentals=0),
        name="features_and_input_grad",
    )(hidden, hidden_edge, grad, grad_edge, k1, k2, b2)


def unpack_kernel(sums_ref, first_ref, second_ref, bias1_ref, bias2_ref, *, scale):
    _, c_in, ch1 = first_ref.shape
    ch2 = second_ref.shape[2]
    three, wide, main = 3 * ch1, 3 * ch2, 7 * ch1
    for a in range(3):
        for b in range(3):
            for c in range(3):
                k = 9 * a + 3 * b + c
                at = a * three + b * ch1
                if at < main:
                    block = sums_ref[at : at + ch1, c * ch2 : (c + 1) * ch2]
                else:
                    at = c * 2 * ch1 + at - main
                    block = sums_ref[at : at + ch1, wide:]
                second_ref[k] = block * scale
                down, right = (main, b * three + c * ch1) if b < 2 or c < 2 else (6 * ch1, wide)
                first_ref[k] = sums_ref[down + a * c_in : down + (a + 1) * c_in, right : right + ch1] * scale
    at = main + 3 * c_in
    bias1_ref[...] = sums_ref[at : at + 1, :ch1] * scale
    bias2_ref[...] = sums_ref[at + 1 : at + 2, :ch2] * scale


def unpack(sums, scale, c_in, ch1, ch2):
    first, bias1, second, bias2 = (
        jax.ShapeDtypeStruct(shape, F32) for shape in ((27, c_in, ch1), (1, ch1), (27, ch1, ch2), (1, ch2))
    )
    first, second, bias1, bias2 = pl.pallas_call(
        functools.partial(unpack_kernel, scale=scale),
        out_shape=(first, second, bias1, bias2),
        name="unpack_sums",
    )(sums)
    first = first.reshape(3, 3, 3, c_in, ch1).transpose(4, 3, 0, 1, 2)
    second = second.reshape(3, 3, 3, ch1, ch2).transpose(4, 3, 0, 1, 2)
    return first, bias1[0], second, bias2[0]


def total_over_devices(sums):
    slabs, tiles = lax.axis_size("gz"), lax.axis_size("xy")

    def exchange(value, axis):
        return lax.all_to_all(value, axis, 0, 0, tiled=True)

    def copies(value, count):
        return jnp.broadcast_to(value[None], (count,) + value.shape)

    part = exchange(sums.reshape(slabs, -1, sums.shape[1]), "gz").sum(0).astype(BF16)
    part = exchange(copies(part, tiles), "xy").astype(F32).sum(0)
    parts = exchange(copies(part, slabs), "gz")
    return parts.reshape(sums.shape)


def shards(loaded_planes, first_kernel, first_bias, second_kernel, second_bias, cotangent):
    channels, _, planes_dev, _, width, depth_y = loaded_planes.shape
    tiles = lax.axis_size("xy")
    slabs = lax.axis_size("gz")
    ch1, ch2 = first_kernel.shape[0], second_kernel.shape[0]
    depth_z = planes_dev * tiles
    k1 = first_kernel.transpose(2, 3, 4, 1, 0).reshape(27, channels, ch1)
    k2 = second_kernel.transpose(2, 3, 4, 1, 0).reshape(27, ch1, ch2)
    g, t = lax.axis_index("gz"), lax.axis_index("xy")
    place = jnp.stack([g == 0, g == slabs - 1, t == 0, t == tiles - 1]).astype(jnp.int32)

    windows = pack(loaded_planes.reshape(channels, width, depth_y), tiles)
    mid = lax.all_to_all(windows, "xy", split_axis=0, concat_axis=0, tiled=True)

    cot = cotangent.reshape(ch2, depth_z // 2, depth_y // 2)
    left, right = shifted(cot, "xy", 1), shifted(cot, "xy", -1)
    raw, shifts, ends, w1, odd, even = prep(left, cot, right, k1, first_bias[None], k2)

    rows = mid.shape[1]
    upward = jnp.concatenate([mid[-2:].reshape(2 * rows, depth_y), ends[3 * ch2 :]], axis=0)
    downward = jnp.concatenate([mid[:2].reshape(2 * rows, depth_y), ends[: 3 * ch2]], axis=0)
    low, high = shifted(upward, "gz", 1), shifted(downward, "gz", -1)
    hidden, grad, first, second = inner(place, mid, raw, shifts, w1)
    hidden_edge, grad_edge, sums = edge(
        place, low, mid, high, ends, odd, even, shifts, w1, hidden, first, second
    )
    sums = total_over_devices(sums)
    features, input_grad = last(hidden, hidden_edge, grad, grad_edge, k1, k2, second_bias[None])
    scale = 1.0 / math.sqrt(slabs * depth_z * width * depth_y)
    first_grad, first_bias_grad, second_grad, second_bias_grad = unpack(sums, scale, channels, ch1, ch2)
    return (
        features[:, :, None, :],
        input_grad.reshape(channels, depth_z, 2, depth_y),
        first_grad,
        first_bias_grad,
        second_grad,
        second_bias_grad,
    )


def solution(mesh):
    return jax.shard_map(
        shards,
        mesh=mesh,
        in_specs=(
            P(None, "gz", None, "xy", None, None),
            P(),
            P(),
            P(),
            P(),
            P(None, "gz", "xy", None),
        ),
        out_specs=(P(None, "gz", "xy", None), P(None, "gz", "xy", None), P(), P(), P(), P()),
        check_vma=False,
    )
```

```python
import functools
import math

import jax
import jax.numpy as jnp
from jax import lax
from jax.experimental import pallas as pl
from jax.experimental.pallas import tpu as pltpu
from jax.sharding import PartitionSpec as P

BF16 = jnp.bfloat16
F32 = jnp.float32
WINDOW = 8
COLUMNS = 4
VMEM_LIMIT = 12 * 1024 * 1024


def shifted(value, axis, steps):
    count = lax.axis_size(axis)
    first, last = (max(0, -steps), min(count, count - steps))
    return lax.ppermute(value, axis, [(source, source + steps) for source in range(first, last)])


def mm(left, right):
    return jnp.dot(left, right, preferred_element_type=F32)


def mm_nt(left, right):
    return lax.dot_general(left, right, (((1,), (1,)), ((), ())), preferred_element_type=F32)


def from_left(value):
    lane = lax.broadcasted_iota(jnp.int32, value.shape, 1)
    return jnp.where(lane == 0, 0.0, pltpu.roll(value, 1, 1))


def from_right(value):
    lane = lax.broadcasted_iota(jnp.int32, value.shape, 1)
    last = value.shape[1] - 1
    return jnp.where(lane == last, 0.0, pltpu.roll(value, last, 1))


def lanes(blocks):
    return blocks[0] if len(blocks) == 1 else jnp.concatenate(blocks, axis=1)


def pack_kernel(planes_ref, out_ref, wide_ref):
    channels, width, _ = planes_ref.shape
    wide_ref[...] = jnp.zeros_like(wide_ref)
    wide_ref[:, 8 : 8 + width, :] = planes_ref[...].astype(F32)
    targets = out_ref.shape[0]
    row = lax.broadcasted_iota(jnp.int32, (WINDOW, out_ref.shape[2]), 0)
    for t in range(targets):
        parts = [wide_ref[i, 6 + 2 * t : 6 + 2 * t + WINDOW, :] for i in range(channels)]
        parts = [jnp.where(row >= WINDOW - 2, 1.0, part) for part in parts]
        out_ref[t] = jnp.concatenate(parts, axis=0).astype(BF16)


def pack(planes, targets):
    channels, width, depth_y = planes.shape
    shape = (targets, channels * WINDOW, depth_y)
    return pl.pallas_call(
        pack_kernel,
        out_shape=jax.ShapeDtypeStruct(shape, BF16),
        scratch_shapes=[pltpu.VMEM((channels, width + 16, depth_y), F32)],
        compiler_params=pltpu.CompilerParams(vmem_limit_bytes=VMEM_LIMIT),
        name="pack_windows",
    )(planes)


def split_bias(bias):
    high = bias.astype(BF16).astype(F32)
    middle = (bias - high).astype(BF16).astype(F32)
    return high, middle, bias - high - middle


def first_matrix(kernel_ref, bias_ref, turned_ref):
    _, c_in, ch1 = kernel_ref.shape
    size = COLUMNS * ch1
    turned_ref[...] = jnp.zeros_like(turned_ref)
    nothing = jnp.zeros((c_in, ch1), F32)

    def block(a, b, c):
        return kernel_ref[9 * a + 3 * b + c].astype(F32) if 0 <= b < 3 and c < 3 else nothing

    for a in range(3):
        for w in range(COLUMNS + 2):
            at = pl.ds(a * c_in * WINDOW + w, c_in, stride=WINDOW)
            for half in range(2):
                blocks = [block(a, w - x, c) for c in (2 * half, 2 * half + 1) for x in range(COLUMNS)]
                turned_ref[half, at, :] = jnp.concatenate(blocks, axis=1)
    for n, part in enumerate(split_bias(bias_ref[...])):
        row = c_in * WINDOW + n * WINDOW + WINDOW - 2
        for x in range(COLUMNS):
            half, right = divmod(size + x * ch1, 128)
            turned_ref[half, row : row + 1, right : right + ch1] = part
    return jnp.concatenate([turned_ref[0].T, turned_ref[1].T], axis=0)[: 3 * size].astype(BF16)


def spread_matrix(kernel_ref, out_ref, row, a, column):
    _, ch1, ch2 = kernel_ref.shape
    for c in range(3):
        for x in range(COLUMNS):
            for q in range(3):
                b = x - 1 - 2 * (q - 1) + 1
                if 0 <= b <= 2:
                    down, right = row + (c * COLUMNS + x) * ch1, column + q * ch2
                    out_ref[down : down + ch1, right : right + ch2] = kernel_ref[9 * a + 3 * b + c]


def unspread(terms):
    size = terms.shape[0] // 3
    return from_right(terms[:size]) + terms[size : 2 * size] + from_left(terms[2 * size :])


def moved_three(value):
    return jnp.concatenate([from_right(value), value, from_left(value)], axis=0).astype(BF16)


def even_plane(pair):
    lane = lax.broadcasted_iota(jnp.int32, pair.shape, 1)
    return jnp.where(lane % 2 == 0, pair, 0.0)


def odd_plane(pair):
    return even_plane(from_right(pair))


def own_kernel(mid_ref, k1_ref, b1_ref, k2_ref, shifts_ref, pairs_ref, w1_ref, odd_ref, even_ref, flat_ref, turned_ref):
    ch2, cells, half_y = mid_ref.shape
    rows = 3 * ch2
    depth_y = 2 * half_y
    spread = (
        2 * lax.broadcasted_iota(jnp.int32, (half_y, depth_y), 0)
        == lax.broadcasted_iota(jnp.int32, (half_y, depth_y), 1)
    ).astype(F32).astype(BF16)
    flat_ref[...] = mid_ref[...].astype(F32).reshape(ch2 * cells, half_y)
    for q in range(cells):
        wide = mm(flat_ref[pl.ds(q, ch2, stride=cells), :].astype(BF16), spread)
        shifts_ref[q * rows : (q + 1) * rows, :] = moved_three(wide)
        if q % 2 == 0:
            first = wide
        else:
            pairs_ref[q // 2 * ch2 : (q // 2 + 1) * ch2, :] = (first + from_left(wide)).astype(BF16)
    w1_ref[...] = first_matrix(k1_ref, b1_ref, turned_ref)
    odd_ref[...] = jnp.zeros_like(odd_ref)
    even_ref[...] = jnp.zeros_like(even_ref)
    spread_matrix(k2_ref, odd_ref, 0, 2, 0)
    spread_matrix(k2_ref, odd_ref, 0, 0, rows)
    spread_matrix(k2_ref, even_ref, 0, 1, 0)


def prepare_own(mid, k1, b1, k2):
    ch2, cells, half_y = mid.shape
    _, c_in, ch1 = k1.shape
    depth_y = 2 * half_y
    size, rows = COLUMNS * ch1, 3 * ch2
    return pl.pallas_call(
        own_kernel,
        out_shape=(
            jax.ShapeDtypeStruct((cells * rows, depth_y), BF16),
            jax.ShapeDtypeStruct((cells // 2 * ch2, depth_y), BF16),
            jax.ShapeDtypeStruct((3 * size, 3 * c_in * WINDOW), BF16),
            jax.ShapeDtypeStruct((3 * size, 2 * rows), BF16),
            jax.ShapeDtypeStruct((3 * size, rows), BF16),
        ),
        scratch_shapes=[
            pltpu.VMEM((ch2 * cells, half_y), F32),
            pltpu.VMEM((2, 3 * c_in * WINDOW, 128), F32),
        ],
        compiler_params=pltpu.CompilerParams(vmem_limit_bytes=VMEM_LIMIT),
        cost_estimate=pl.CostEstimate(flops=100_000_000, bytes_accessed=2_000_000, transcendentals=0),
        name="spread_cotangent",
    )(mid, k1, b1, k2)


def spread_columns(left_ref, shifts_ref, right_ref, wide_ref, cells):
    rows = wide_ref.shape[0] // cells
    ch2 = rows // 3
    for k in range(cells // 2):
        sides = [ref[k * ch2 : (k + 1) * ch2, :].astype(F32) for ref in (left_ref, right_ref)]
        for n, plane in enumerate((even_plane, odd_plane)):
            at = (2 * k + n) * rows
            wide_ref[at : at + ch2, :] = plane(sides[0]).astype(BF16)
            wide_ref[at + ch2 : at + 2 * ch2, :] = shifts_ref[at + ch2 : at + 2 * ch2, :]
            wide_ref[at + 2 * ch2 : at + rows, :] = plane(sides[1]).astype(BF16)


def rim_columns(ref, plane, first_row):
    ch2 = (ref.shape[0] - first_row) // 3
    left, own, right = (ref[first_row + k * ch2 : first_row + (k + 1) * ch2, :] for k in range(3))
    left, right = (plane(pair.astype(F32)).astype(BF16) for pair in (left, right))
    return jnp.concatenate([left, own, right], axis=0)


def raw_levels(wide_ref, odd_ref, even_ref, raw_ref, cells):
    size = even_ref.shape[0] // 3
    rows = wide_ref.shape[0] // cells
    depth_y = wide_ref.shape[1]

    def store(z, terms):
        raw_ref[(z - 1) * size : z * size, :] = unspread(terms)

    for m in range(0, cells - 1, 2):
        group = [k for k in (m, m + 1) if k < cells - 1]
        odd = mm(odd_ref[...], lanes([wide_ref[k * rows : (k + 2) * rows, :] for k in group]))
        even = mm(even_ref[...], lanes([wide_ref[(k + 1) * rows : (k + 2) * rows, :] for k in group]))
        for n, k in enumerate(group):
            store(2 * k + 1, odd[:, n * depth_y : (n + 1) * depth_y])
            store(2 * k + 2, even[:, n * depth_y : (n + 1) * depth_y])


def activate(groups, plane, raw, place_ref, w1_ref, depth_z, store):
    size = w1_ref.shape[0] // 3
    ch1 = size // COLUMNS
    at_first_z, at_last_z, at_first_x, at_last_x = (place_ref[k] for k in range(4))
    depth_y = plane(groups[0][0]).shape[1]
    row = lax.broadcasted_iota(jnp.int32, (size, depth_y), 0)
    outside = ((row < ch1) & (at_first_x != 0)) | ((row >= 3 * ch1) & (at_last_x != 0))
    inside = jnp.where(outside, 0.0, 1.0)
    for group in groups:
        source = lanes([jnp.concatenate([plane(z + a) for a in (-1, 0, 1)], axis=0) for z in group])
        products = mm(w1_ref[...], source)
        for n, z in enumerate(group):
            terms = products[:, n * depth_y : (n + 1) * depth_y]
            pre = from_left(terms[:size]) + terms[size : 2 * size] + from_right(terms[2 * size :])
            sigma = 1.0 / (1.0 + jnp.exp(-pre))
            keep = inside
            if z == -1:
                keep = inside * jnp.where(at_first_z != 0, 0.0, 1.0)
            if z == depth_z:
                keep = inside * jnp.where(at_last_z != 0, 0.0, 1.0)
            kept = sigma * keep
            store(z, (pre * kept)[: 3 * ch1], raw(z) * (kept * (1.0 + pre * (1.0 - sigma))))


def side_by_side(grad, ch1):
    own = grad[ch1 : 3 * ch1]
    parts = [from_right(own), own, from_left(own)]
    sides = [part[x * ch1 : (x + 1) * ch1] for x in range(2) for part in parts]
    return jnp.concatenate(sides, axis=0).astype(BF16)


def first_terms(levels, plane, moved):
    source = lanes([jnp.concatenate([plane(z + a) for a in (-1, 0, 1)], axis=0) for z in levels])
    return mm_nt(source, lanes([moved(z) for z in levels]))


def second_terms(cells, hidden, shifts):
    both = lanes([jnp.concatenate([hidden(2 * q + 1), hidden(2 * q + 2)], axis=0) for q in cells])
    size = both.shape[0] // 2
    upper = mm_nt(both, lanes([shifts(q + 1) for q in cells]))
    return upper, mm_nt(both[:size], lanes([shifts(q) for q in cells]))


def store_level(hidden_ref, grad_ref, at, hidden, grad, ch1):
    size = COLUMNS * ch1
    hidden_ref[at * size : at * size + 3 * ch1, :] = hidden.astype(BF16)
    hidden_ref[at * size + 3 * ch1 : (at + 1) * size, :] = jnp.ones((ch1, hidden.shape[1]), BF16)
    grad_ref[at * size : (at + 1) * size, :] = grad.astype(BF16)


def inner_kernel(
    place_ref,
    mid_ref,
    left_ref,
    shifts_ref,
    right_ref,
    odd_ref,
    even_ref,
    w1_ref,
    wide_ref,
    hidden_ref,
    grad_ref,
    first_ref,
    second_ref,
    raw_ref,
    moved_ref,
):
    depth_z = mid_ref.shape[0]
    size = w1_ref.shape[0] // 3
    ch1 = size // COLUMNS
    levels = list(range(1, depth_z - 1))
    six = 6 * ch1
    three = shifts_ref.shape[0] // (depth_z // 2)
    spread_columns(left_ref, shifts_ref, right_ref, wide_ref, depth_z // 2)
    raw_levels(wide_ref, odd_ref, even_ref, raw_ref, depth_z // 2)

    def store(z, hidden, grad):
        store_level(hidden_ref, grad_ref, z - 1, hidden, grad, ch1)
        moved_ref[(z - 1) * six : z * six, :] = side_by_side(grad, ch1)

    def plane(z):
        return mid_ref[z]

    def raw(z):
        return raw_ref[(z - 1) * size : z * size, :]

    def moved(z):
        return moved_ref[(z - 1) * six : z * six, :]

    def hidden(z):
        return hidden_ref[(z - 1) * size : z * size, :]

    def shifts(q):
        return shifts_ref[q * three : (q + 1) * three, :]

    pairs = [levels[k : k + 2] for k in range(0, len(levels), 2)]
    activate(pairs, plane, raw, place_ref, w1_ref, depth_z, store)
    total = None
    for pair in pairs:
        term = first_terms(pair, plane, moved)
        total = term if total is None else total + term
    first_ref[...] = total
    upper = lower = None
    cells = list(range(depth_z // 2 - 1))
    for k in range(0, len(cells), 2):
        add_upper, add_lower = second_terms(cells[k : k + 2], hidden, shifts)
        upper = add_upper if upper is None else upper + add_upper
        lower = add_lower if lower is None else lower + add_lower
    second_ref[: 2 * size, :] = upper
    second_ref[2 * size :, :] = lower


def edge_kernel(
    place_ref,
    mid_ref,
    high_ref,
    wide_ref,
    odd_ref,
    even_ref,
    shifts_ref,
    w1_ref,
    first_ref,
    second_ref,
    hidden_ref,
    grad_ref,
    sums_ref,
    begin_ref,
    moved_ref,
    fold_ref,
):
    depth_z, rows, depth_y = mid_ref.shape
    size = w1_ref.shape[0] // 3
    ch1 = size // COLUMNS
    cells = depth_z // 2
    spread_rows = wide_ref.shape[0] // cells
    ch2 = spread_rows // 3
    end = wide_ref[(cells - 1) * spread_rows :, :]
    above = rim_columns(high_ref, even_plane, 2 * rows)
    even = mm(even_ref[...], lanes([wide_ref[:spread_rows, :], above]))
    raws = {
        0: unspread(even[:, :depth_y]),
        depth_z - 1: unspread(mm(odd_ref[...], jnp.concatenate([end, above], axis=0))),
        depth_z: unspread(even[:, depth_y:]),
    }
    places = {depth_z - 1: 0, depth_z: 1, 0: 2}
    six = 6 * ch1

    def plane(z):
        if z < 0:
            return jnp.zeros((rows, depth_y), BF16)
        if z >= depth_z:
            return high_ref[(z - depth_z) * rows : (z - depth_z + 1) * rows, :]
        return mid_ref[z]

    def store(z, hidden, grad):
        at = places[z]
        if z > 0:
            store_level(hidden_ref, grad_ref, at, hidden, grad, ch1)
        else:
            begin_ref[: 3 * ch1, :] = hidden.astype(BF16)
            begin_ref[3 * ch1 :, :] = jnp.ones((ch1, depth_y), BF16)
        moved_ref[at * six : (at + 1) * six, :] = side_by_side(grad, ch1)

    def moved(z):
        return moved_ref[places[z] * six : (places[z] + 1) * six, :]

    def hidden(z):
        return hidden_ref[places[z] * size : (places[z] + 1) * size, :]

    def shifts(q):
        if q < cells:
            return shifts_ref[q * spread_rows : (q + 1) * spread_rows, :]
        return moved_three(above[ch2 : 2 * ch2].astype(F32))

    groups = [[depth_z - 1, depth_z], [0]]
    activate(groups, plane, lambda z: raws[z], place_ref, w1_ref, depth_z, store)
    at_bottom = jnp.where(place_ref[0] != 0, 1.0, 0.0)
    first = first_ref[...] + first_terms([depth_z - 1, depth_z], plane, moved)
    first = first + at_bottom * first_terms([0], plane, moved)
    upper, lower = second_terms([cells - 1], hidden, shifts)
    bottom = at_bottom * mm_nt(begin_ref[...], shifts(0))
    second = second_ref[...] + jnp.concatenate([upper[:size], upper[size:] + bottom, lower], axis=0)
    three = 3 * ch1
    wide = 3 * ch2
    main = 7 * ch1
    for a in range(2):
        sums_ref[a * three : (a + 1) * three, :wide] = second[a * size : a * size + three]
    sums_ref[2 * three : main, :wide] = second[2 * size : 2 * size + ch1]
    rest = second[2 * size + ch1 : 2 * size + three]
    sums_ref[6 * ch1 : main, wide:] = jnp.zeros((ch1, 128 - wide), F32)
    sums_ref[main : main + ch1, :] = jnp.zeros((ch1, 128), F32)
    for c in range(3):
        sums_ref[c * 2 * ch1 : (c + 1) * 2 * ch1, wide:] = rest[:, c * ch2 : (c + 1) * ch2]
    count = first.shape[0]
    fold_ref[...] = first[:, :three] + pltpu.roll(first, count - 1, 0)[:, three:]
    groups = count // WINDOW
    for b in range(3):
        block = fold_ref[pl.ds(b + 1, groups, stride=WINDOW), :]
        if b < 2:
            sums_ref[main : main + groups, b * three : (b + 1) * three] = block
        else:
            sums_ref[main : main + groups, wide : wide + ch1] = block[:, :ch1]
            sums_ref[main : main + groups, wide + ch1 :] = block[:, ch1 : 2 * ch1]
            sums_ref[6 * ch1 : 6 * ch1 + groups, wide : wide + ch1] = block[:, 2 * ch1 :]
    at = count // 3 + WINDOW - 2
    sums_ref[main + groups : main + groups + 1, :ch1] = fold_ref[at : at + 1, ch1 : 2 * ch1]
    at = size + three
    sums_ref[main + groups + 1 : main + groups + 2, :ch2] = second[at : at + 1, ch2 : 2 * ch2]


def inner(place, mid, left, shifts, right, odd, even, w1):
    depth_z, rows, depth_y = mid.shape
    size = w1.shape[0] // 3
    ch1 = size // COLUMNS
    ch2 = shifts.shape[0] // (3 * (depth_z // 2))
    vmem = pl.BlockSpec(memory_space=pltpu.VMEM)
    count = depth_z - 2
    return pl.pallas_call(
        inner_kernel,
        in_specs=[pl.BlockSpec(memory_space=pltpu.SMEM)] + [vmem] * 7,
        out_specs=(vmem,) * 5,
        out_shape=(
            jax.ShapeDtypeStruct(shifts.shape, BF16),
            jax.ShapeDtypeStruct((count * size, depth_y), BF16),
            jax.ShapeDtypeStruct((count * size, depth_y), BF16),
            jax.ShapeDtypeStruct((3 * rows, 6 * ch1), F32),
            jax.ShapeDtypeStruct((3 * size, 3 * ch2), F32),
        ),
        scratch_shapes=[pltpu.VMEM((count * size, depth_y), F32), pltpu.VMEM((count * 6 * ch1, depth_y), BF16)],
        compiler_params=pltpu.CompilerParams(vmem_limit_bytes=VMEM_LIMIT),
        cost_estimate=pl.CostEstimate(flops=800_000_000, bytes_accessed=10_000_000, transcendentals=500_000),
        name="inner_levels",
    )(place, mid, left, shifts, right, odd, even, w1)


def edge(place, mid, high, wide, odd, even, shifts, w1, first, second):
    _, rows, depth_y = mid.shape
    size = w1.shape[0] // 3
    ch1 = size // COLUMNS
    vmem = pl.BlockSpec(memory_space=pltpu.VMEM)
    return pl.pallas_call(
        edge_kernel,
        in_specs=[pl.BlockSpec(memory_space=pltpu.SMEM)] + [vmem] * 9,
        out_specs=(vmem,) * 3,
        out_shape=(
            jax.ShapeDtypeStruct((2 * size, depth_y), BF16),
            jax.ShapeDtypeStruct((2 * size, depth_y), BF16),
            jax.ShapeDtypeStruct((8 * ch1, 128), F32),
        ),
        scratch_shapes=[
            pltpu.VMEM((size, depth_y), BF16),
            pltpu.VMEM((3 * 6 * ch1, depth_y), BF16),
            pltpu.VMEM((3 * rows, 3 * ch1), F32),
        ],
        compiler_params=pltpu.CompilerParams(vmem_limit_bytes=VMEM_LIMIT),
        name="edge_levels_and_sums",
    )(place, mid, high, wide, odd, even, shifts, w1, first, second)


def last_kernel(
    place_ref,
    low_ref,
    mid_ref,
    wide_ref,
    w1_ref,
    odd_ref,
    even_ref,
    hidden_ref,
    grad_ref,
    hidden_edge_ref,
    grad_edge_ref,
    k1_ref,
    k2_ref,
    b2_ref,
    feat_ref,
    gin_ref,
    hidden_low_ref,
    grad_low_ref,
    featw_ref,
    ginw_ref,
    turned_ref,
    w4_ref,
):
    ch2, depth_q, half_y = feat_ref.shape
    c_in, _, depth_y = gin_ref.shape
    depth_z, rows, _ = mid_ref.shape
    size = hidden_edge_ref.shape[0] // 2
    ch1 = size // COLUMNS

    def plane(z):
        return low_ref[(z + 2) * rows : (z + 3) * rows, :] if z < 0 else mid_ref[z]

    below, here = rim_columns(low_ref, odd_plane, 2 * rows), wide_ref[: 3 * ch2, :]
    raws = {
        -1: unspread(mm(odd_ref[...], jnp.concatenate([below, here], axis=0))),
        0: unspread(mm(even_ref[...], here)),
    }

    def store(z, hidden, grad):
        store_level(hidden_low_ref, grad_low_ref, z + 1, hidden, grad, ch1)

    activate([[-1, 0]], plane, lambda z: raws[z], place_ref, w1_ref, depth_z, store)

    def hidden(z):
        if z < 1:
            return hidden_low_ref[(z + 1) * size : (z + 2) * size, :]
        if z < depth_z - 1:
            return hidden_ref[(z - 1) * size : z * size, :]
        return hidden_edge_ref[(z - depth_z + 1) * size : (z - depth_z + 2) * size, :]

    def grad(z):
        if z < 1:
            return grad_low_ref[(z + 1) * size : (z + 2) * size, :]
        if z < depth_z - 1:
            return grad_ref[(z - 1) * size : z * size, :]
        return grad_edge_ref[(z - depth_z + 1) * size : (z - depth_z + 2) * size, :]

    def window(level, z):
        return jnp.concatenate([level(z + a) for a in (-1, 0, 1)], axis=0)

    turned_ref[...] = jnp.zeros_like(turned_ref)
    w4_ref[...] = jnp.zeros_like(w4_ref)
    for a in range(3):
        for b in range(3):
            for c in range(3):
                k = 9 * a + 3 * b + c
                down = a * size + b * ch1
                turned_ref[down : down + ch1, c * ch2 : (c + 1) * ch2] = k2_ref[k].astype(F32)
                for x in range(2):
                    down, right = (c * 2 + x) * c_in, (2 - a) * size + (x + 2 - b) * ch1
                    w4_ref[down : down + c_in, right : right + ch1] = k1_ref[k].astype(F32)
    for n, part in enumerate(split_bias(b2_ref[...])):
        row = size + 3 * ch1 + n
        turned_ref[row : row + 1, ch2 : 2 * ch2] = part
    w2 = turned_ref[...].T[: 3 * ch2].astype(BF16)
    w4 = w4_ref[...].astype(BF16)
    pick = (
        lax.broadcasted_iota(jnp.int32, (depth_y, half_y), 0)
        == 2 * lax.broadcasted_iota(jnp.int32, (depth_y, half_y), 1)
    ).astype(F32).astype(BF16)

    for q in range(0, depth_q, 2):
        source = lanes([window(hidden, 2 * k) for k in (q, q + 1)])
        products = mm(w2, source)
        for n in range(2):
            terms = products[:, n * depth_y : (n + 1) * depth_y]
            full = from_left(terms[:ch2]) + terms[ch2 : 2 * ch2] + from_right(terms[2 * ch2 :])
            featw_ref[pl.ds(q + n, ch2, stride=depth_q), :] = mm(full.astype(BF16), pick)
    feat_ref[...] = featw_ref[...].reshape(feat_ref.shape).astype(BF16)

    two = 2 * c_in
    for z in range(0, depth_z, 2):
        source = lanes([window(grad, k) for k in (z, z + 1)])
        products = mm(w4, source)
        for n in range(2):
            terms = products[:, n * depth_y : (n + 1) * depth_y]
            full = from_right(terms[:two]) + terms[two : 2 * two] + from_left(terms[2 * two :])
            for x in range(2):
                at = pl.ds(2 * (z + n) + x, c_in, stride=2 * depth_z)
                ginw_ref[at, :] = full[x * c_in : (x + 1) * c_in]
    gin_ref[...] = ginw_ref[...].reshape(gin_ref.shape).astype(BF16)


def last(place, low, mid, wide, w1, odd, even, inner_values, edge_values, k1, k2, b2):
    depth_z, _, depth_y = mid.shape
    _, c_in, ch1 = k1.shape
    ch2 = k2.shape[2]
    size = COLUMNS * ch1
    depth_q = depth_z // 2
    vmem = pl.BlockSpec(memory_space=pltpu.VMEM)
    return pl.pallas_call(
        last_kernel,
        in_specs=[pl.BlockSpec(memory_space=pltpu.SMEM)] + [vmem] * 13,
        out_specs=(vmem, vmem),
        out_shape=(
            jax.ShapeDtypeStruct((ch2, depth_q, depth_y // 2), BF16),
            jax.ShapeDtypeStruct((c_in, 2 * depth_z, depth_y), BF16),
        ),
        scratch_shapes=[
            pltpu.VMEM((2 * size, depth_y), BF16),
            pltpu.VMEM((2 * size, depth_y), BF16),
            pltpu.VMEM((ch2 * depth_q, depth_y // 2), F32),
            pltpu.VMEM((c_in * 2 * depth_z, depth_y), F32),
            pltpu.VMEM((3 * size, 128), F32),
            pltpu.VMEM((3 * 2 * c_in, 3 * size), F32),
        ],
        compiler_params=pltpu.CompilerParams(vmem_limit_bytes=VMEM_LIMIT),
        cost_estimate=pl.CostEstimate(flops=800_000_000, bytes_accessed=10_000_000, transcendentals=0),
        name="features_and_input_grad",
    )(place, low, mid, wide, w1, odd, even, *inner_values, *edge_values, k1, k2, b2)


def unpack_kernel(sums_ref, first_ref, second_ref, bias1_ref, bias2_ref, *, scale):
    _, c_in, ch1 = first_ref.shape
    ch2 = second_ref.shape[2]
    three, wide, main = 3 * ch1, 3 * ch2, 7 * ch1
    for a in range(3):
        for b in range(3):
            for c in range(3):
                k = 9 * a + 3 * b + c
                at = a * three + b * ch1
                if at < main:
                    block = sums_ref[at : at + ch1, c * ch2 : (c + 1) * ch2]
                else:
                    at = c * 2 * ch1 + at - main
                    block = sums_ref[at : at + ch1, wide:]
                second_ref[k] = block * scale
                down, right = (main, b * three + c * ch1) if b < 2 or c < 2 else (6 * ch1, wide)
                first_ref[k] = sums_ref[down + a * c_in : down + (a + 1) * c_in, right : right + ch1] * scale
    at = main + 3 * c_in
    bias1_ref[...] = sums_ref[at : at + 1, :ch1] * scale
    bias2_ref[...] = sums_ref[at + 1 : at + 2, :ch2] * scale


def unpack(sums, scale, c_in, ch1, ch2):
    first, bias1, second, bias2 = (
        jax.ShapeDtypeStruct(shape, F32) for shape in ((27, c_in, ch1), (1, ch1), (27, ch1, ch2), (1, ch2))
    )
    first, second, bias1, bias2 = pl.pallas_call(
        functools.partial(unpack_kernel, scale=scale),
        in_specs=[pl.BlockSpec(memory_space=pltpu.VMEM)],
        out_shape=(first, second, bias1, bias2),
        name="unpack_sums",
    )(sums)
    first = first.reshape(3, 3, 3, c_in, ch1).transpose(4, 3, 0, 1, 2)
    second = second.reshape(3, 3, 3, ch1, ch2).transpose(4, 3, 0, 1, 2)
    return first, bias1[0], second, bias2[0]


def exchange(value, axis):
    return lax.all_to_all(value, axis, 0, 0, tiled=True)


def copies(value, count):
    return jnp.broadcast_to(value[None], (count,) + value.shape)


def shards(loaded_planes, first_kernel, first_bias, second_kernel, second_bias, cotangent):
    channels, _, planes_dev, _, width, depth_y = loaded_planes.shape
    tiles = lax.axis_size("xy")
    slabs = lax.axis_size("gz")
    ch1, ch2 = first_kernel.shape[0], second_kernel.shape[0]
    depth_z = planes_dev * tiles
    k1 = first_kernel.transpose(2, 3, 4, 1, 0).reshape(27, channels, ch1)
    k2 = second_kernel.transpose(2, 3, 4, 1, 0).reshape(27, ch1, ch2)
    g, t = lax.axis_index("gz"), lax.axis_index("xy")
    place = jnp.stack([g == 0, g == slabs - 1, t == 0, t == tiles - 1]).astype(jnp.int32)

    windows = pack(loaded_planes.reshape(channels, width, depth_y), tiles)
    mid = lax.all_to_all(windows, "xy", split_axis=0, concat_axis=0, tiled=True)

    cot = cotangent.reshape(ch2, depth_z // 2, depth_y // 2)
    shifts, pairs, w1, odd, even = prepare_own(cot, k1, first_bias[None], k2)
    left, right = shifted(pairs, "xy", 1), shifted(pairs, "xy", -1)
    mid, left, right = lax.optimization_barrier((mid, left, right))

    rows = mid.shape[1]
    downward = [mid[:2].reshape(2 * rows, depth_y), left[:ch2], shifts[ch2 : 2 * ch2], right[:ch2]]
    high = shifted(jnp.concatenate(downward, axis=0), "gz", -1)
    wide, *inner_values, first, second = inner(place, mid, left, shifts, right, odd, even, w1)
    *edge_values, sums = edge(place, mid, high, wide, odd, even, shifts, w1, first, second)

    part = exchange(sums.reshape(slabs, -1, sums.shape[1]), "gz").sum(0).astype(BF16)
    upward = [mid[-2:].reshape(2 * rows, depth_y), left[-ch2:], shifts[-2 * ch2 : -ch2], right[-ch2:]]
    part, upward = lax.optimization_barrier((part, jnp.concatenate(upward, axis=0)))
    low = shifted(upward, "gz", 1)
    part = exchange(copies(part, tiles), "xy").astype(F32).sum(0)
    part, low = lax.optimization_barrier((part, low))
    sums = exchange(copies(part, slabs), "gz").reshape(sums.shape)
    features, input_grad = last(
        place, low, mid, wide, w1, odd, even, inner_values, edge_values, k1, k2, second_bias[None]
    )
    scale = 1.0 / math.sqrt(slabs * depth_z * width * depth_y)
    first_grad, first_bias_grad, second_grad, second_bias_grad = unpack(sums, scale, channels, ch1, ch2)
    return (
        features[:, :, None, :],
        input_grad.reshape(channels, depth_z, 2, depth_y),
        first_grad,
        first_bias_grad,
        second_grad,
        second_bias_grad,
    )


def solution(mesh):
    return jax.shard_map(
        shards,
        mesh=mesh,
        in_specs=(
            P(None, "gz", None, "xy", None, None),
            P(),
            P(),
            P(),
            P(),
            P(None, "gz", "xy", None),
        ),
        out_specs=(P(None, "gz", "xy", None), P(None, "gz", "xy", None), P(), P(), P(), P()),
        check_vma=False,
    )
```

```python
import functools
import math

import jax
import jax.numpy as jnp
from jax import lax
from jax.experimental import pallas as pl
from jax.experimental.pallas import tpu as pltpu
from jax.sharding import PartitionSpec as P

BF16 = jnp.bfloat16
F32 = jnp.float32
WINDOW = 8
COLUMNS = 4
VMEM_LIMIT = 12 * 1024 * 1024


def shifted(value, axis, steps):
    count = lax.axis_size(axis)
    first, last = (max(0, -steps), min(count, count - steps))
    return lax.ppermute(value, axis, [(source, source + steps) for source in range(first, last)])


def mm(left, right):
    return jnp.dot(left, right, preferred_element_type=F32)


def mm_nt(left, right):
    return lax.dot_general(left, right, (((1,), (1,)), ((), ())), preferred_element_type=F32)


def from_left(value):
    lane = lax.broadcasted_iota(jnp.int32, value.shape, 1)
    return jnp.where(lane == 0, 0.0, pltpu.roll(value, 1, 1))


def from_right(value):
    lane = lax.broadcasted_iota(jnp.int32, value.shape, 1)
    last = value.shape[1] - 1
    return jnp.where(lane == last, 0.0, pltpu.roll(value, last, 1))


def lanes(blocks):
    return blocks[0] if len(blocks) == 1 else jnp.concatenate(blocks, axis=1)


def pack_kernel(planes_ref, out_ref, wide_ref):
    channels, width, _ = planes_ref.shape
    wide_ref[...] = jnp.zeros_like(wide_ref)
    wide_ref[:, 8 : 8 + width, :] = planes_ref[...].astype(F32)
    targets = out_ref.shape[0]
    row = lax.broadcasted_iota(jnp.int32, (WINDOW, out_ref.shape[2]), 0)
    for t in range(targets):
        parts = [wide_ref[i, 6 + 2 * t : 6 + 2 * t + WINDOW, :] for i in range(channels)]
        parts = [jnp.where(row >= WINDOW - 2, 1.0, part) for part in parts]
        out_ref[t] = jnp.concatenate(parts, axis=0).astype(BF16)


def pack(planes, targets):
    channels, width, depth_y = planes.shape
    shape = (targets, channels * WINDOW, depth_y)
    return pl.pallas_call(
        pack_kernel,
        out_shape=jax.ShapeDtypeStruct(shape, BF16),
        scratch_shapes=[pltpu.VMEM((channels, width + 16, depth_y), F32)],
        compiler_params=pltpu.CompilerParams(vmem_limit_bytes=VMEM_LIMIT),
        name="pack_windows",
    )(planes)


def split_bias(bias):
    high = bias.astype(BF16).astype(F32)
    middle = (bias - high).astype(BF16).astype(F32)
    return high, middle, bias - high - middle


def first_matrix(kernel_ref, bias_ref, turned_ref):
    _, c_in, ch1 = kernel_ref.shape
    size = COLUMNS * ch1
    turned_ref[...] = jnp.zeros_like(turned_ref)
    nothing = jnp.zeros((c_in, ch1), F32)

    def block(a, b, c):
        return kernel_ref[9 * a + 3 * b + c].astype(F32) if 0 <= b < 3 and c < 3 else nothing

    for a in range(3):
        for w in range(COLUMNS + 2):
            at = pl.ds(a * c_in * WINDOW + w, c_in, stride=WINDOW)
            for half in range(2):
                blocks = [block(a, w - x, c) for c in (2 * half, 2 * half + 1) for x in range(COLUMNS)]
                turned_ref[half, at, :] = jnp.concatenate(blocks, axis=1)
    for n, part in enumerate(split_bias(bias_ref[...])):
        row = c_in * WINDOW + n * WINDOW + WINDOW - 2
        for x in range(COLUMNS):
            half, right = divmod(size + x * ch1, 128)
            turned_ref[half, row : row + 1, right : right + ch1] = part
    return jnp.concatenate([turned_ref[0].T, turned_ref[1].T], axis=0)[: 3 * size].astype(BF16)


def spread_matrix(kernel_ref, out_ref, row, a, column):
    _, ch1, ch2 = kernel_ref.shape
    for c in range(3):
        for x in range(COLUMNS):
            for q in range(3):
                b = x - 1 - 2 * (q - 1) + 1
                if 0 <= b <= 2:
                    down, right = row + (c * COLUMNS + x) * ch1, column + q * ch2
                    out_ref[down : down + ch1, right : right + ch2] = kernel_ref[9 * a + 3 * b + c]


def unspread(terms):
    size = terms.shape[0] // 3
    return from_right(terms[:size]) + terms[size : 2 * size] + from_left(terms[2 * size :])


def moved_three(value):
    return jnp.concatenate([from_right(value), value, from_left(value)], axis=0).astype(BF16)


def even_plane(pair):
    lane = lax.broadcasted_iota(jnp.int32, pair.shape, 1)
    return jnp.where(lane % 2 == 0, pair, 0.0)


def odd_plane(pair):
    return even_plane(from_right(pair))


def second_matrix(kernel_ref, bias_ref, turned_ref):
    _, ch1, ch2 = kernel_ref.shape
    size = COLUMNS * ch1
    turned_ref[...] = jnp.zeros_like(turned_ref)
    for a in range(3):
        for b in range(3):
            for c in range(3):
                at = a * size + b * ch1
                turned_ref[at : at + ch1, c * ch2 : (c + 1) * ch2] = kernel_ref[9 * a + 3 * b + c].astype(F32)
    for n, part in enumerate(split_bias(bias_ref[...])):
        row = size + 3 * ch1 + n
        turned_ref[row : row + 1, ch2 : 2 * ch2] = part
    return turned_ref[...].T[: 3 * ch2].astype(BF16)


def back_matrix(kernel_ref, flat_ref):
    _, c_in, ch1 = kernel_ref.shape
    size = COLUMNS * ch1
    flat_ref[...] = jnp.zeros_like(flat_ref)
    for a in range(3):
        for b in range(3):
            for c in range(3):
                for x in range(2):
                    down, right = (c * 2 + x) * c_in, (2 - a) * size + (x + 2 - b) * ch1
                    block = kernel_ref[9 * a + 3 * b + c].astype(F32)
                    flat_ref[down : down + c_in, right : right + ch1] = block
    return flat_ref[...].astype(BF16)


def own_kernel(
    mid_ref,
    k1_ref,
    b1_ref,
    k2_ref,
    b2_ref,
    shifts_ref,
    pairs_ref,
    w1_ref,
    odd_ref,
    even_ref,
    w2_ref,
    w4_ref,
    flat_ref,
    turned_ref,
    turned2_ref,
    flat4_ref,
):
    ch2, cells, half_y = mid_ref.shape
    rows = 3 * ch2
    depth_y = 2 * half_y
    spread = (
        2 * lax.broadcasted_iota(jnp.int32, (half_y, depth_y), 0)
        == lax.broadcasted_iota(jnp.int32, (half_y, depth_y), 1)
    ).astype(F32).astype(BF16)
    flat_ref[...] = mid_ref[...].astype(F32).reshape(ch2 * cells, half_y)
    for q in range(cells):
        wide = mm(flat_ref[pl.ds(q, ch2, stride=cells), :].astype(BF16), spread)
        shifts_ref[q * rows : (q + 1) * rows, :] = moved_three(wide)
        if q % 2 == 0:
            first = wide
        else:
            pairs_ref[q // 2 * ch2 : (q // 2 + 1) * ch2, :] = (first + from_left(wide)).astype(BF16)
    w1_ref[...] = first_matrix(k1_ref, b1_ref, turned_ref)
    odd_ref[...] = jnp.zeros_like(odd_ref)
    even_ref[...] = jnp.zeros_like(even_ref)
    spread_matrix(k2_ref, odd_ref, 0, 2, 0)
    spread_matrix(k2_ref, odd_ref, 0, 0, rows)
    spread_matrix(k2_ref, even_ref, 0, 1, 0)
    w2_ref[...] = second_matrix(k2_ref, b2_ref, turned2_ref)
    w4_ref[...] = back_matrix(k1_ref, flat4_ref)


def prepare_own(mid, k1, b1, k2, b2):
    ch2, cells, half_y = mid.shape
    _, c_in, ch1 = k1.shape
    depth_y = 2 * half_y
    size, rows = COLUMNS * ch1, 3 * ch2
    return pl.pallas_call(
        own_kernel,
        out_shape=(
            jax.ShapeDtypeStruct((cells * rows, depth_y), BF16),
            jax.ShapeDtypeStruct((cells // 2 * ch2, depth_y), BF16),
            jax.ShapeDtypeStruct((3 * size, 3 * c_in * WINDOW), BF16),
            jax.ShapeDtypeStruct((3 * size, 2 * rows), BF16),
            jax.ShapeDtypeStruct((3 * size, rows), BF16),
            jax.ShapeDtypeStruct((rows, 3 * size), BF16),
            jax.ShapeDtypeStruct((6 * c_in, 3 * size), BF16),
        ),
        scratch_shapes=[
            pltpu.VMEM((ch2 * cells, half_y), F32),
            pltpu.VMEM((2, 3 * c_in * WINDOW, 128), F32),
            pltpu.VMEM((3 * size, 128), F32),
            pltpu.VMEM((6 * c_in, 3 * size), F32),
        ],
        compiler_params=pltpu.CompilerParams(vmem_limit_bytes=VMEM_LIMIT),
        cost_estimate=pl.CostEstimate(flops=100_000_000, bytes_accessed=2_000_000, transcendentals=0),
        name="spread_cotangent",
    )(mid, k1, b1, k2, b2)


def spread_columns(shifts_ref, right_ref, wide_ref, cells):
    rows = wide_ref.shape[0] // cells
    ch2 = rows // 3
    for k in range(cells // 2):
        pair = right_ref[k * ch2 : (k + 1) * ch2, :].astype(F32)
        for n, plane in enumerate((even_plane(pair), odd_plane(pair))):
            at = (2 * k + n) * rows
            wide_ref[at : at + ch2, :] = jnp.zeros((ch2, pair.shape[1]), BF16)
            wide_ref[at + ch2 : at + 2 * ch2, :] = shifts_ref[at + ch2 : at + 2 * ch2, :]
            wide_ref[at + 2 * ch2 : at + rows, :] = plane.astype(BF16)


def raw_levels(wide_ref, odd_ref, even_ref, raw_ref, cells):
    size = even_ref.shape[0] // 3
    rows = wide_ref.shape[0] // cells
    depth_y = wide_ref.shape[1]

    def store(z, terms):
        raw_ref[(z - 1) * size : z * size, :] = unspread(terms)

    for m in range(0, cells - 1, 2):
        group = [k for k in (m, m + 1) if k < cells - 1]
        odd = mm(odd_ref[...], lanes([wide_ref[k * rows : (k + 2) * rows, :] for k in group]))
        even = mm(even_ref[...], lanes([wide_ref[(k + 1) * rows : (k + 2) * rows, :] for k in group]))
        for n, k in enumerate(group):
            store(2 * k + 1, odd[:, n * depth_y : (n + 1) * depth_y])
            store(2 * k + 2, even[:, n * depth_y : (n + 1) * depth_y])


def activate(groups, plane, raw, place_ref, w1_ref, depth_z, store):
    size = w1_ref.shape[0] // 3
    ch1 = size // COLUMNS
    at_first_z, at_last_z, at_first_x, at_last_x = (place_ref[k] for k in range(4))
    depth_y = plane(groups[0][0]).shape[1]
    row = lax.broadcasted_iota(jnp.int32, (size, depth_y), 0)
    outside = ((row < ch1) & (at_first_x != 0)) | ((row >= 3 * ch1) & (at_last_x != 0))
    inside = jnp.where(outside, 0.0, 1.0)
    for group in groups:
        source = lanes([jnp.concatenate([plane(z + a) for a in (-1, 0, 1)], axis=0) for z in group])
        products = mm(w1_ref[...], source)
        for n, z in enumerate(group):
            terms = products[:, n * depth_y : (n + 1) * depth_y]
            pre = from_left(terms[:size]) + terms[size : 2 * size] + from_right(terms[2 * size :])
            sigma = 1.0 / (1.0 + jnp.exp(-pre))
            keep = inside
            if z == -1:
                keep = inside * jnp.where(at_first_z != 0, 0.0, 1.0)
            if z == depth_z:
                keep = inside * jnp.where(at_last_z != 0, 0.0, 1.0)
            kept = sigma * keep
            slope = kept * (1.0 + pre * (1.0 - sigma))
            store(z, (pre * kept)[: 3 * ch1], raw(z) * slope, slope)


def side_by_side(grad, ch1):
    own = grad[ch1 : 3 * ch1]
    parts = [from_right(own), own, from_left(own)]
    sides = [part[x * ch1 : (x + 1) * ch1] for x in range(2) for part in parts]
    return jnp.concatenate(sides, axis=0).astype(BF16)


def first_terms(levels, plane, moved):
    source = lanes([jnp.concatenate([plane(z + a) for a in (-1, 0, 1)], axis=0) for z in levels])
    return mm_nt(source, lanes([moved(z) for z in levels]))


def second_terms(cells, hidden, shifts):
    both = lanes([jnp.concatenate([hidden(2 * q + 1), hidden(2 * q + 2)], axis=0) for q in cells])
    size = both.shape[0] // 2
    upper = mm_nt(both, lanes([shifts(q + 1) for q in cells]))
    return upper, mm_nt(both[:size], lanes([shifts(q) for q in cells]))


def store_level(hidden_ref, grad_ref, at, hidden, grad, ch1):
    size = COLUMNS * ch1
    hidden_ref[at * size : at * size + 3 * ch1, :] = hidden.astype(BF16)
    hidden_ref[at * size + 3 * ch1 : (at + 1) * size, :] = jnp.ones((ch1, hidden.shape[1]), BF16)
    grad_ref[at * size : (at + 1) * size, :] = grad.astype(BF16)


def inner_kernel(
    place_ref,
    mid_ref,
    shifts_ref,
    right_ref,
    odd_ref,
    even_ref,
    w1_ref,
    wide_ref,
    hidden_ref,
    grad_ref,
    slope_ref,
    first_ref,
    second_ref,
    raw_ref,
    moved_ref,
):
    depth_z = mid_ref.shape[0]
    size = w1_ref.shape[0] // 3
    ch1 = size // COLUMNS
    levels = list(range(1, depth_z - 1))
    six = 6 * ch1
    three = shifts_ref.shape[0] // (depth_z // 2)
    spread_columns(shifts_ref, right_ref, wide_ref, depth_z // 2)
    raw_levels(wide_ref, odd_ref, even_ref, raw_ref, depth_z // 2)

    def store(z, hidden, grad, slope):
        store_level(hidden_ref, grad_ref, z - 1, hidden, grad, ch1)
        slope_ref[(z - 1) * ch1 : z * ch1, :] = slope[:ch1]
        moved_ref[(z - 1) * six : z * six, :] = side_by_side(grad, ch1)

    def plane(z):
        return mid_ref[z]

    def raw(z):
        return raw_ref[(z - 1) * size : z * size, :]

    def moved(z):
        return moved_ref[(z - 1) * six : z * six, :]

    def hidden(z):
        return hidden_ref[(z - 1) * size : z * size, :]

    def shifts(q):
        return shifts_ref[q * three : (q + 1) * three, :]

    pairs = [levels[k : k + 2] for k in range(0, len(levels), 2)]
    activate(pairs, plane, raw, place_ref, w1_ref, depth_z, store)
    total = None
    for pair in pairs:
        term = first_terms(pair, plane, moved)
        total = term if total is None else total + term
    first_ref[...] = total
    upper = lower = None
    cells = list(range(depth_z // 2 - 1))
    for k in range(0, len(cells), 2):
        add_upper, add_lower = second_terms(cells[k : k + 2], hidden, shifts)
        upper = add_upper if upper is None else upper + add_upper
        lower = add_lower if lower is None else lower + add_lower
    second_ref[: 2 * size, :] = upper
    second_ref[2 * size :, :] = lower


def edge_kernel(
    place_ref,
    mid_ref,
    high_ref,
    wide_ref,
    odd_ref,
    even_ref,
    shifts_ref,
    w1_ref,
    first_ref,
    second_ref,
    hidden_ref,
    grad_ref,
    slope_ref,
    sums_ref,
    begin_ref,
    moved_ref,
    fold_ref,
):
    depth_z, rows, depth_y = mid_ref.shape
    size = w1_ref.shape[0] // 3
    ch1 = size // COLUMNS
    cells = depth_z // 2
    spread_rows = wide_ref.shape[0] // cells
    ch2 = spread_rows // 3
    end = wide_ref[(cells - 1) * spread_rows :, :]
    right = even_plane(high_ref[2 * rows + ch2 :, :].astype(F32)).astype(BF16)
    above = jnp.concatenate([jnp.zeros((ch2, depth_y), BF16), high_ref[2 * rows : 2 * rows + ch2, :], right], axis=0)
    even = mm(even_ref[...], lanes([wide_ref[:spread_rows, :], above]))
    raws = {
        0: unspread(even[:, :depth_y]),
        depth_z - 1: unspread(mm(odd_ref[...], jnp.concatenate([end, above], axis=0))),
        depth_z: unspread(even[:, depth_y:]),
    }
    places = {depth_z - 1: 0, depth_z: 1, 0: 2}
    six = 6 * ch1

    def plane(z):
        if z < 0:
            return jnp.zeros((rows, depth_y), BF16)
        if z >= depth_z:
            return high_ref[(z - depth_z) * rows : (z - depth_z + 1) * rows, :]
        return mid_ref[z]

    def store(z, hidden, grad, slope):
        at = places[z]
        if z > 0:
            store_level(hidden_ref, grad_ref, at, hidden, grad, ch1)
            slope_ref[at * ch1 : (at + 1) * ch1, :] = slope[:ch1]
        else:
            begin_ref[: 3 * ch1, :] = hidden.astype(BF16)
            begin_ref[3 * ch1 :, :] = jnp.ones((ch1, depth_y), BF16)
        moved_ref[at * six : (at + 1) * six, :] = side_by_side(grad, ch1)

    def moved(z):
        return moved_ref[places[z] * six : (places[z] + 1) * six, :]

    def hidden(z):
        return hidden_ref[places[z] * size : (places[z] + 1) * size, :]

    def shifts(q):
        if q < cells:
            return shifts_ref[q * spread_rows : (q + 1) * spread_rows, :]
        return moved_three(above[ch2 : 2 * ch2].astype(F32))

    groups = [[depth_z - 1, depth_z], [0]]
    activate(groups, plane, lambda z: raws[z], place_ref, w1_ref, depth_z, store)
    at_bottom = jnp.where(place_ref[0] != 0, 1.0, 0.0)
    first = first_ref[...] + first_terms([depth_z - 1, depth_z], plane, moved)
    first = first + at_bottom * first_terms([0], plane, moved)
    upper, lower = second_terms([cells - 1], hidden, shifts)
    bottom = at_bottom * mm_nt(begin_ref[...], shifts(0))
    second = second_ref[...] + jnp.concatenate([upper[:size], upper[size:] + bottom, lower], axis=0)
    three = 3 * ch1
    wide = 3 * ch2
    main = 7 * ch1
    for a in range(2):
        sums_ref[a * three : (a + 1) * three, :wide] = second[a * size : a * size + three]
    sums_ref[2 * three : main, :wide] = second[2 * size : 2 * size + ch1]
    rest = second[2 * size + ch1 : 2 * size + three]
    sums_ref[6 * ch1 : main, wide:] = jnp.zeros((ch1, 128 - wide), F32)
    sums_ref[main : main + ch1, :] = jnp.zeros((ch1, 128), F32)
    for c in range(3):
        sums_ref[c * 2 * ch1 : (c + 1) * 2 * ch1, wide:] = rest[:, c * ch2 : (c + 1) * ch2]
    count = first.shape[0]
    fold_ref[...] = first[:, :three] + pltpu.roll(first, count - 1, 0)[:, three:]
    groups = count // WINDOW
    for b in range(3):
        block = fold_ref[pl.ds(b + 1, groups, stride=WINDOW), :]
        if b < 2:
            sums_ref[main : main + groups, b * three : (b + 1) * three] = block
        else:
            sums_ref[main : main + groups, wide : wide + ch1] = block[:, :ch1]
            sums_ref[main : main + groups, wide + ch1 :] = block[:, ch1 : 2 * ch1]
            sums_ref[6 * ch1 : 6 * ch1 + groups, wide : wide + ch1] = block[:, 2 * ch1 :]
    at = count // 3 + WINDOW - 2
    sums_ref[main + groups : main + groups + 1, :ch1] = fold_ref[at : at + 1, ch1 : 2 * ch1]
    at = size + three
    sums_ref[main + groups + 1 : main + groups + 2, :ch2] = second[at : at + 1, ch2 : 2 * ch2]


def inner(place, mid, shifts, right, odd, even, w1):
    depth_z, rows, depth_y = mid.shape
    size = w1.shape[0] // 3
    ch1 = size // COLUMNS
    ch2 = shifts.shape[0] // (3 * (depth_z // 2))
    vmem = pl.BlockSpec(memory_space=pltpu.VMEM)
    count = depth_z - 2
    return pl.pallas_call(
        inner_kernel,
        in_specs=[pl.BlockSpec(memory_space=pltpu.SMEM)] + [vmem] * 6,
        out_specs=(vmem,) * 6,
        out_shape=(
            jax.ShapeDtypeStruct(shifts.shape, BF16),
            jax.ShapeDtypeStruct((count * size, depth_y), BF16),
            jax.ShapeDtypeStruct((count * size, depth_y), BF16),
            jax.ShapeDtypeStruct((count * ch1, depth_y), F32),
            jax.ShapeDtypeStruct((3 * rows, 6 * ch1), F32),
            jax.ShapeDtypeStruct((3 * size, 3 * ch2), F32),
        ),
        scratch_shapes=[pltpu.VMEM((count * size, depth_y), F32), pltpu.VMEM((count * 6 * ch1, depth_y), BF16)],
        compiler_params=pltpu.CompilerParams(vmem_limit_bytes=VMEM_LIMIT),
        cost_estimate=pl.CostEstimate(flops=0, bytes_accessed=0, transcendentals=0),
        name="inner_levels",
    )(place, mid, shifts, right, odd, even, w1)


def edge(place, mid, high, wide, odd, even, shifts, w1, first, second):
    _, rows, depth_y = mid.shape
    size = w1.shape[0] // 3
    ch1 = size // COLUMNS
    vmem = pl.BlockSpec(memory_space=pltpu.VMEM)
    return pl.pallas_call(
        edge_kernel,
        in_specs=[pl.BlockSpec(memory_space=pltpu.SMEM)] + [vmem] * 9,
        out_specs=(vmem,) * 4,
        out_shape=(
            jax.ShapeDtypeStruct((2 * size, depth_y), BF16),
            jax.ShapeDtypeStruct((2 * size, depth_y), BF16),
            jax.ShapeDtypeStruct((2 * ch1, depth_y), F32),
            jax.ShapeDtypeStruct((8 * ch1, 128), F32),
        ),
        scratch_shapes=[
            pltpu.VMEM((size, depth_y), BF16),
            pltpu.VMEM((3 * 6 * ch1, depth_y), BF16),
            pltpu.VMEM((3 * rows, 3 * ch1), F32),
        ],
        compiler_params=pltpu.CompilerParams(vmem_limit_bytes=VMEM_LIMIT),
        name="edge_levels_and_sums",
    )(place, mid, high, wide, odd, even, shifts, w1, first, second)


def last_kernel(
    place_ref,
    low_ref,
    mid_ref,
    high_ref,
    left_ref,
    corner_ref,
    wide_ref,
    w1_ref,
    odd_ref,
    even_ref,
    hidden_ref,
    grad_ref,
    slope_ref,
    hidden_edge_ref,
    grad_edge_ref,
    slope_edge_ref,
    w2_ref,
    w4_ref,
    feat_ref,
    gin_ref,
    leftw_ref,
    hidden_low_ref,
    grad_low_ref,
    fixed_ref,
    featw_ref,
    ginw_ref,
):
    ch2, depth_q, half_y = feat_ref.shape
    c_in, _, depth_y = gin_ref.shape
    depth_z, rows, _ = mid_ref.shape
    size = hidden_edge_ref.shape[0] // 2
    ch1 = size // COLUMNS
    spread_rows = 3 * ch2

    def spread(q, count):
        left = leftw_ref[(q + 1) * ch2 : (q + 2) * ch2, :]
        if q < 0:
            rest = low_ref[2 * rows + ch2 : 2 * rows + count * ch2, :]
        elif q >= depth_q:
            rest = high_ref[2 * rows : 2 * rows + ch2, :]
        else:
            rest = wide_ref[q * spread_rows + ch2 : q * spread_rows + count * ch2, :]
        return jnp.concatenate([left, rest], axis=0)

    def plane(z):
        return low_ref[(z + 2) * rows : (z + 3) * rows, :] if z < 0 else mid_ref[z]

    leftw_ref[:ch2, :] = odd_plane(low_ref[2 * rows : 2 * rows + ch2, :].astype(F32)).astype(BF16)
    for k in range(depth_q // 2):
        pair = left_ref[k * ch2 : (k + 1) * ch2, :].astype(F32)
        at = (2 * k + 1) * ch2
        leftw_ref[at : at + ch2, :] = even_plane(pair).astype(BF16)
        leftw_ref[at + ch2 : at + 2 * ch2, :] = odd_plane(pair).astype(BF16)
    leftw_ref[(depth_q + 1) * ch2 :, :] = even_plane(corner_ref[...].astype(F32)).astype(BF16)
    below, here = spread(-1, 3), spread(0, 3)
    raws = {
        -1: unspread(mm(odd_ref[...], jnp.concatenate([below, here], axis=0))),
        0: unspread(mm(even_ref[...], here)),
    }

    def store(z, hidden, grad, slope):
        store_level(hidden_low_ref, grad_low_ref, z + 1, hidden, grad, ch1)

    activate([[-1, 0]], plane, lambda z: raws[z], place_ref, w1_ref, depth_z, store)

    two = 2 * ch2
    odd = jnp.concatenate([odd_ref[c * size : c * size + ch1, :] for c in range(3)], axis=0)
    odd = jnp.concatenate([odd[:, :two], odd[:, spread_rows : spread_rows + two]], axis=1)
    even = jnp.concatenate([even_ref[c * size : c * size + ch1, :] for c in range(3)], axis=0)[:, :two]

    def fix(z, raw):
        if z < depth_z - 1:
            slope = slope_ref[(z - 1) * ch1 : z * ch1, :]
        else:
            slope = slope_edge_ref[(z - depth_z + 1) * ch1 : (z - depth_z + 2) * ch1, :]
        fixed_ref[(z - 1) * ch1 : z * ch1, :] = (raw * slope).astype(BF16)

    for q in range(0, depth_q, 2):
        cells = [spread(k, 2) for k in (q, q + 1, q + 2)]
        pairs = lanes([jnp.concatenate(cells[n : n + 2], axis=0) for n in range(2)])
        odds, evens = mm(odd, pairs), mm(even, lanes(cells[1:]))
        for n in range(2):
            at = slice(n * depth_y, (n + 1) * depth_y)
            fix(2 * (q + n) + 1, unspread(odds[:, at]))
            fix(2 * (q + n) + 2, unspread(evens[:, at]))

    def hidden(z):
        if z < 1:
            return hidden_low_ref[(z + 1) * size : (z + 2) * size, :]
        if z < depth_z - 1:
            return hidden_ref[(z - 1) * size : z * size, :]
        return hidden_edge_ref[(z - depth_z + 1) * size : (z - depth_z + 2) * size, :]

    def grad(z):
        if z < 1:
            return grad_low_ref[(z + 1) * size : (z + 2) * size, :]
        if z < depth_z - 1:
            rest = grad_ref[(z - 1) * size + ch1 : z * size, :]
        else:
            rest = grad_edge_ref[(z - depth_z + 1) * size + ch1 : (z - depth_z + 2) * size, :]
        return jnp.concatenate([fixed_ref[(z - 1) * ch1 : z * ch1, :], rest], axis=0)

    def window(level, z):
        return jnp.concatenate([level(z + a) for a in (-1, 0, 1)], axis=0)

    pick = (
        lax.broadcasted_iota(jnp.int32, (depth_y, half_y), 0)
        == 2 * lax.broadcasted_iota(jnp.int32, (depth_y, half_y), 1)
    ).astype(F32).astype(BF16)

    for q in range(0, depth_q, 2):
        source = lanes([window(hidden, 2 * k) for k in (q, q + 1)])
        products = mm(w2_ref[...], source)
        for n in range(2):
            terms = products[:, n * depth_y : (n + 1) * depth_y]
            full = from_left(terms[:ch2]) + terms[ch2 : 2 * ch2] + from_right(terms[2 * ch2 :])
            featw_ref[pl.ds(q + n, ch2, stride=depth_q), :] = mm(full.astype(BF16), pick)
    feat_ref[...] = featw_ref[...].reshape(feat_ref.shape).astype(BF16)

    two = 2 * c_in
    for z in range(0, depth_z, 2):
        source = lanes([window(grad, k) for k in (z, z + 1)])
        products = mm(w4_ref[...], source)
        for n in range(2):
            terms = products[:, n * depth_y : (n + 1) * depth_y]
            full = from_right(terms[:two]) + terms[two : 2 * two] + from_left(terms[2 * two :])
            for x in range(2):
                at = pl.ds(2 * (z + n) + x, c_in, stride=2 * depth_z)
                ginw_ref[at, :] = full[x * c_in : (x + 1) * c_in]
    gin_ref[...] = ginw_ref[...].reshape(gin_ref.shape).astype(BF16)


def last(place, low, mid, high, left, corner, wide, w1, odd, even, inner_values, edge_values, w2, w4):
    depth_z, _, depth_y = mid.shape
    ch2, c_in = w2.shape[0] // 3, w4.shape[0] // 6
    size = w1.shape[0] // 3
    ch1 = size // COLUMNS
    depth_q = depth_z // 2
    vmem = pl.BlockSpec(memory_space=pltpu.VMEM)
    return pl.pallas_call(
        last_kernel,
        in_specs=[pl.BlockSpec(memory_space=pltpu.SMEM)] + [vmem] * 17,
        out_specs=(vmem, vmem),
        out_shape=(
            jax.ShapeDtypeStruct((ch2, depth_q, depth_y // 2), BF16),
            jax.ShapeDtypeStruct((c_in, 2 * depth_z, depth_y), BF16),
        ),
        scratch_shapes=[
            pltpu.VMEM(((depth_q + 2) * ch2, depth_y), BF16),
            pltpu.VMEM((2 * size, depth_y), BF16),
            pltpu.VMEM((2 * size, depth_y), BF16),
            pltpu.VMEM((depth_z * ch1, depth_y), BF16),
            pltpu.VMEM((ch2 * depth_q, depth_y // 2), F32),
            pltpu.VMEM((c_in * 2 * depth_z, depth_y), F32),
        ],
        compiler_params=pltpu.CompilerParams(vmem_limit_bytes=VMEM_LIMIT),
        cost_estimate=pl.CostEstimate(flops=800_000_000, bytes_accessed=10_000_000, transcendentals=0),
        name="features_and_input_grad",
    )(place, low, mid, high, left, corner, wide, w1, odd, even, *inner_values, *edge_values, w2, w4)


def unpack_kernel(sums_ref, first_ref, second_ref, bias1_ref, bias2_ref, *, scale):
    _, c_in, ch1 = first_ref.shape
    ch2 = second_ref.shape[2]
    three, wide, main = 3 * ch1, 3 * ch2, 7 * ch1
    for a in range(3):
        for b in range(3):
            for c in range(3):
                k = 9 * a + 3 * b + c
                at = a * three + b * ch1
                if at < main:
                    block = sums_ref[at : at + ch1, c * ch2 : (c + 1) * ch2]
                else:
                    at = c * 2 * ch1 + at - main
                    block = sums_ref[at : at + ch1, wide:]
                second_ref[k] = block * scale
                down, right = (main, b * three + c * ch1) if b < 2 or c < 2 else (6 * ch1, wide)
                first_ref[k] = sums_ref[down + a * c_in : down + (a + 1) * c_in, right : right + ch1] * scale
    at = main + 3 * c_in
    bias1_ref[...] = sums_ref[at : at + 1, :ch1] * scale
    bias2_ref[...] = sums_ref[at + 1 : at + 2, :ch2] * scale


def unpack(sums, scale, c_in, ch1, ch2):
    first, bias1, second, bias2 = (
        jax.ShapeDtypeStruct(shape, F32) for shape in ((27, c_in, ch1), (1, ch1), (27, ch1, ch2), (1, ch2))
    )
    first, second, bias1, bias2 = pl.pallas_call(
        functools.partial(unpack_kernel, scale=scale),
        in_specs=[pl.BlockSpec(memory_space=pltpu.VMEM)],
        out_shape=(first, second, bias1, bias2),
        compiler_params=pltpu.CompilerParams(vmem_limit_bytes=VMEM_LIMIT),
        name="unpack_sums",
    )(sums)
    first = first.reshape(3, 3, 3, c_in, ch1).transpose(4, 3, 0, 1, 2)
    second = second.reshape(3, 3, 3, ch1, ch2).transpose(4, 3, 0, 1, 2)
    return first, bias1[0], second, bias2[0]


def exchange(value, axis):
    return lax.all_to_all(value, axis, 0, 0, tiled=True)


def copies(value, count):
    return jnp.broadcast_to(value[None], (count,) + value.shape)


def shards(loaded_planes, first_kernel, first_bias, second_kernel, second_bias, cotangent):
    channels, _, planes_dev, _, width, depth_y = loaded_planes.shape
    tiles = lax.axis_size("xy")
    slabs = lax.axis_size("gz")
    ch1, ch2 = first_kernel.shape[0], second_kernel.shape[0]
    depth_z = planes_dev * tiles
    k1 = first_kernel.transpose(2, 3, 4, 1, 0).reshape(27, channels, ch1)
    k2 = second_kernel.transpose(2, 3, 4, 1, 0).reshape(27, ch1, ch2)
    g, t = lax.axis_index("gz"), lax.axis_index("xy")
    place = jnp.stack([g == 0, g == slabs - 1, t == 0, t == tiles - 1]).astype(jnp.int32)

    windows = pack(loaded_planes.reshape(channels, width, depth_y), tiles)
    mid = lax.all_to_all(windows, "xy", split_axis=0, concat_axis=0, tiled=True)

    cot = cotangent.reshape(ch2, depth_z // 2, depth_y // 2)
    shifts, pairs, w1, odd, even, w2, w4 = prepare_own(cot, k1, first_bias[None], k2, second_bias[None])
    left, right = shifted(pairs, "xy", 1), shifted(pairs, "xy", -1)
    mid, right = lax.optimization_barrier((mid, right))

    rows = mid.shape[1]
    downward = jnp.concatenate([mid[:2].reshape(2 * rows, depth_y), shifts[ch2 : 2 * ch2], right[:ch2]], axis=0)
    high = shifted(downward, "gz", -1)
    wide, *inner_values, first, second = inner(place, mid, shifts, right, odd, even, w1)
    high, left = lax.optimization_barrier((high, left))
    *edge_values, sums = edge(place, mid, high, wide, odd, even, shifts, w1, first, second)

    part = exchange(sums.reshape(slabs, -1, sums.shape[1]), "gz").sum(0).astype(BF16)
    upward = [mid[-2:].reshape(2 * rows, depth_y), left[-ch2:], wide[-2 * ch2 :]]
    part, upward, corner = lax.optimization_barrier((part, jnp.concatenate(upward, axis=0), left[:ch2]))
    low, corner = shifted(upward, "gz", 1), shifted(corner, "gz", -1)
    part = exchange(copies(part, tiles), "xy").astype(F32).sum(0)
    part, low, corner = lax.optimization_barrier((part, low, corner))
    sums = exchange(copies(part, slabs), "gz").reshape(sums.shape)
    features, input_grad = last(
        place, low, mid, high, left, corner, wide, w1, odd, even, inner_values, edge_values, w2, w4
    )
    scale = 1.0 / math.sqrt(slabs * depth_z * width * depth_y)
    first_grad, first_bias_grad, second_grad, second_bias_grad = unpack(sums, scale, channels, ch1, ch2)
    return (
        features[:, :, None, :],
        input_grad.reshape(channels, depth_z, 2, depth_y),
        first_grad,
        first_bias_grad,
        second_grad,
        second_bias_grad,
    )


def solution(mesh):
    return jax.shard_map(
        shards,
        mesh=mesh,
        in_specs=(
            P(None, "gz", None, "xy", None, None),
            P(),
            P(),
            P(),
            P(),
            P(None, "gz", "xy", None),
        ),
        out_specs=(P(None, "gz", "xy", None), P(None, "gz", "xy", None), P(), P(), P(), P()),
        check_vma=False,
    )
```

```python
import functools
import math

import jax
import jax.numpy as jnp
from jax import lax
from jax.experimental import pallas as pl
from jax.experimental.pallas import tpu as pltpu
from jax.sharding import PartitionSpec as P

BF16 = jnp.bfloat16
F32 = jnp.float32
WINDOW = 8
COLUMNS = 4
VMEM_LIMIT = 12 * 1024 * 1024


def shifted(value, axis, steps):
    count = lax.axis_size(axis)
    first, last = (max(0, -steps), min(count, count - steps))
    return lax.ppermute(value, axis, [(source, source + steps) for source in range(first, last)])


def mm(left, right):
    return jnp.dot(left, right, preferred_element_type=F32)


def mm_nt(left, right):
    return lax.dot_general(left, right, (((1,), (1,)), ((), ())), preferred_element_type=F32)


def from_left(value):
    lane = lax.broadcasted_iota(jnp.int32, value.shape, 1)
    return jnp.where(lane == 0, 0.0, pltpu.roll(value, 1, 1))


def from_right(value):
    lane = lax.broadcasted_iota(jnp.int32, value.shape, 1)
    last = value.shape[1] - 1
    return jnp.where(lane == last, 0.0, pltpu.roll(value, last, 1))


def lanes(blocks):
    return blocks[0] if len(blocks) == 1 else jnp.concatenate(blocks, axis=1)


def pack_kernel(planes_ref, out_ref, wide_ref):
    channels, width, _ = planes_ref.shape
    wide_ref[...] = jnp.zeros_like(wide_ref)
    wide_ref[:, 8 : 8 + width, :] = planes_ref[...].astype(F32)
    targets = out_ref.shape[0]
    row = lax.broadcasted_iota(jnp.int32, (WINDOW, out_ref.shape[2]), 0)
    for t in range(targets):
        parts = [wide_ref[i, 6 + 2 * t : 6 + 2 * t + WINDOW, :] for i in range(channels)]
        parts = [jnp.where(row >= WINDOW - 2, 1.0, part) for part in parts]
        out_ref[t] = jnp.concatenate(parts, axis=0).astype(BF16)


def pack(planes, targets):
    channels, width, depth_y = planes.shape
    shape = (targets, channels * WINDOW, depth_y)
    return pl.pallas_call(
        pack_kernel,
        out_shape=jax.ShapeDtypeStruct(shape, BF16),
        scratch_shapes=[pltpu.VMEM((channels, width + 16, depth_y), F32)],
        compiler_params=pltpu.CompilerParams(vmem_limit_bytes=VMEM_LIMIT),
        name="pack_windows",
    )(planes)


def split_bias(bias):
    high = bias.astype(BF16).astype(F32)
    middle = (bias - high).astype(BF16).astype(F32)
    return high, middle, bias - high - middle


def first_matrix(kernel_ref, bias_ref, turned_ref):
    _, c_in, ch1 = kernel_ref.shape
    size = COLUMNS * ch1
    turned_ref[...] = jnp.zeros_like(turned_ref)
    nothing = jnp.zeros((c_in, ch1), F32)

    def block(a, b, c):
        return kernel_ref[9 * a + 3 * b + c].astype(F32) if 0 <= b < 3 and c < 3 else nothing

    for a in range(3):
        for w in range(COLUMNS + 2):
            at = pl.ds(a * c_in * WINDOW + w, c_in, stride=WINDOW)
            for half in range(2):
                blocks = [block(a, w - x, c) for c in (2 * half, 2 * half + 1) for x in range(COLUMNS)]
                turned_ref[half, at, :] = jnp.concatenate(blocks, axis=1)
    for n, part in enumerate(split_bias(bias_ref[...])):
        row = c_in * WINDOW + n * WINDOW + WINDOW - 2
        for x in range(COLUMNS):
            half, right = divmod(size + x * ch1, 128)
            turned_ref[half, row : row + 1, right : right + ch1] = part
    return jnp.concatenate([turned_ref[0].T, turned_ref[1].T], axis=0)[: 3 * size].astype(BF16)


def spread_matrix(kernel_ref, out_ref, row, a, column):
    _, ch1, ch2 = kernel_ref.shape
    for c in range(3):
        for x in range(COLUMNS):
            for q in range(3):
                b = x - 1 - 2 * (q - 1) + 1
                if 0 <= b <= 2:
                    down, right = row + (c * COLUMNS + x) * ch1, column + q * ch2
                    out_ref[down : down + ch1, right : right + ch2] = kernel_ref[9 * a + 3 * b + c]


def unspread(terms):
    size = terms.shape[0] // 3
    return from_right(terms[:size]) + terms[size : 2 * size] + from_left(terms[2 * size :])


def moved_three(value):
    return jnp.concatenate([from_right(value), value, from_left(value)], axis=0).astype(BF16)


def even_plane(pair):
    lane = lax.broadcasted_iota(jnp.int32, pair.shape, 1)
    return jnp.where(lane % 2 == 0, pair, 0.0)


def odd_plane(pair):
    return even_plane(from_right(pair))


def second_matrix(kernel_ref, bias_ref, turned_ref):
    _, ch1, ch2 = kernel_ref.shape
    size = COLUMNS * ch1
    turned_ref[...] = jnp.zeros_like(turned_ref)
    for a in range(3):
        for b in range(3):
            for c in range(3):
                at = a * size + b * ch1
                turned_ref[at : at + ch1, c * ch2 : (c + 1) * ch2] = kernel_ref[9 * a + 3 * b + c].astype(F32)
    for n, part in enumerate(split_bias(bias_ref[...])):
        row = size + 3 * ch1 + n
        turned_ref[row : row + 1, ch2 : 2 * ch2] = part
    return turned_ref[...].T[: 3 * ch2].astype(BF16)


def back_matrix(kernel_ref, flat_ref):
    _, c_in, ch1 = kernel_ref.shape
    size = COLUMNS * ch1
    flat_ref[...] = jnp.zeros_like(flat_ref)
    for a in range(3):
        for b in range(3):
            for c in range(3):
                for x in range(2):
                    down, right = (c * 2 + x) * c_in, (2 - a) * size + (x + 2 - b) * ch1
                    block = kernel_ref[9 * a + 3 * b + c].astype(F32)
                    flat_ref[down : down + c_in, right : right + ch1] = block
    return flat_ref[...].astype(BF16)


def own_kernel(
    mid_ref,
    k1_ref,
    b1_ref,
    k2_ref,
    b2_ref,
    shifts_ref,
    pairs_ref,
    w1_ref,
    odd_ref,
    even_ref,
    w2_ref,
    w4_ref,
    flat_ref,
    turned_ref,
    turned2_ref,
    flat4_ref,
):
    ch2, cells, half_y = mid_ref.shape
    rows = 3 * ch2
    depth_y = 2 * half_y
    spread = (
        2 * lax.broadcasted_iota(jnp.int32, (half_y, depth_y), 0)
        == lax.broadcasted_iota(jnp.int32, (half_y, depth_y), 1)
    ).astype(F32).astype(BF16)
    flat_ref[...] = mid_ref[...].astype(F32).reshape(ch2 * cells, half_y)
    for q in range(cells):
        wide = mm(flat_ref[pl.ds(q, ch2, stride=cells), :].astype(BF16), spread)
        shifts_ref[q * rows : (q + 1) * rows, :] = moved_three(wide)
        if q % 2 == 0:
            first = wide
        else:
            pairs_ref[q // 2 * ch2 : (q // 2 + 1) * ch2, :] = (first + from_left(wide)).astype(BF16)
    w1_ref[...] = first_matrix(k1_ref, b1_ref, turned_ref)
    odd_ref[...] = jnp.zeros_like(odd_ref)
    even_ref[...] = jnp.zeros_like(even_ref)
    spread_matrix(k2_ref, odd_ref, 0, 2, 0)
    spread_matrix(k2_ref, odd_ref, 0, 0, rows)
    spread_matrix(k2_ref, even_ref, 0, 1, 0)
    w2_ref[...] = second_matrix(k2_ref, b2_ref, turned2_ref)
    w4_ref[...] = back_matrix(k1_ref, flat4_ref)


def prepare_own(mid, k1, b1, k2, b2):
    ch2, cells, half_y = mid.shape
    _, c_in, ch1 = k1.shape
    depth_y = 2 * half_y
    size, rows = COLUMNS * ch1, 3 * ch2
    return pl.pallas_call(
        own_kernel,
        out_shape=(
            jax.ShapeDtypeStruct((cells * rows, depth_y), BF16),
            jax.ShapeDtypeStruct((cells // 2 * ch2, depth_y), BF16),
            jax.ShapeDtypeStruct((3 * size, 3 * c_in * WINDOW), BF16),
            jax.ShapeDtypeStruct((3 * size, 2 * rows), BF16),
            jax.ShapeDtypeStruct((3 * size, rows), BF16),
            jax.ShapeDtypeStruct((rows, 3 * size), BF16),
            jax.ShapeDtypeStruct((6 * c_in, 3 * size), BF16),
        ),
        scratch_shapes=[
            pltpu.VMEM((ch2 * cells, half_y), F32),
            pltpu.VMEM((2, 3 * c_in * WINDOW, 128), F32),
            pltpu.VMEM((3 * size, 128), F32),
            pltpu.VMEM((6 * c_in, 3 * size), F32),
        ],
        compiler_params=pltpu.CompilerParams(vmem_limit_bytes=VMEM_LIMIT),
        cost_estimate=pl.CostEstimate(flops=100_000_000, bytes_accessed=2_000_000, transcendentals=0),
        name="spread_cotangent",
    )(mid, k1, b1, k2, b2)


def spread_columns(shifts_ref, right_ref, wide_ref, cells):
    rows = wide_ref.shape[0] // cells
    ch2 = rows // 3
    for k in range(cells // 2):
        pair = right_ref[k * ch2 : (k + 1) * ch2, :].astype(F32)
        for n, plane in enumerate((even_plane(pair), odd_plane(pair))):
            at = (2 * k + n) * rows
            wide_ref[at : at + ch2, :] = jnp.zeros((ch2, pair.shape[1]), BF16)
            wide_ref[at + ch2 : at + 2 * ch2, :] = shifts_ref[at + ch2 : at + 2 * ch2, :]
            wide_ref[at + 2 * ch2 : at + rows, :] = plane.astype(BF16)


def raw_levels(wide_ref, odd_ref, even_ref, raw_ref, cells):
    size = even_ref.shape[0] // 3
    rows = wide_ref.shape[0] // cells
    depth_y = wide_ref.shape[1]

    def store(z, terms):
        raw_ref[(z - 1) * size : z * size, :] = unspread(terms)

    for m in range(0, cells - 1, 2):
        group = [k for k in (m, m + 1) if k < cells - 1]
        odd = mm(odd_ref[...], lanes([wide_ref[k * rows : (k + 2) * rows, :] for k in group]))
        even = mm(even_ref[...], lanes([wide_ref[(k + 1) * rows : (k + 2) * rows, :] for k in group]))
        for n, k in enumerate(group):
            store(2 * k + 1, odd[:, n * depth_y : (n + 1) * depth_y])
            store(2 * k + 2, even[:, n * depth_y : (n + 1) * depth_y])


def activate(groups, plane, raw, place_ref, w1_ref, depth_z, store):
    size = w1_ref.shape[0] // 3
    ch1 = size // COLUMNS
    at_first_z, at_last_z, at_first_x, at_last_x = (place_ref[k] for k in range(4))
    depth_y = plane(groups[0][0]).shape[1]
    row = lax.broadcasted_iota(jnp.int32, (size, depth_y), 0)
    outside = ((row < ch1) & (at_first_x != 0)) | ((row >= 3 * ch1) & (at_last_x != 0))
    inside = jnp.where(outside, 0.0, 1.0)
    for group in groups:
        source = lanes([jnp.concatenate([plane(z + a) for a in (-1, 0, 1)], axis=0) for z in group])
        products = mm(w1_ref[...], source)
        for n, z in enumerate(group):
            terms = products[:, n * depth_y : (n + 1) * depth_y]
            pre = from_left(terms[:size]) + terms[size : 2 * size] + from_right(terms[2 * size :])
            sigma = 1.0 / (1.0 + jnp.exp(-pre))
            keep = inside
            if z == -1:
                keep = inside * jnp.where(at_first_z != 0, 0.0, 1.0)
            if z == depth_z:
                keep = inside * jnp.where(at_last_z != 0, 0.0, 1.0)
            kept = sigma * keep
            slope = kept * (1.0 + pre * (1.0 - sigma))
            store(z, (pre * kept)[: 3 * ch1], raw(z) * slope, slope)


def side_by_side(grad, ch1):
    own = grad[ch1 : 3 * ch1]
    parts = [from_right(own), own, from_left(own)]
    sides = [part[x * ch1 : (x + 1) * ch1] for x in range(2) for part in parts]
    return jnp.concatenate(sides, axis=0).astype(BF16)


def first_terms(levels, plane, moved):
    source = lanes([jnp.concatenate([plane(z + a) for a in (-1, 0, 1)], axis=0) for z in levels])
    return mm_nt(source, lanes([moved(z) for z in levels]))


def second_terms(cells, hidden, shifts):
    both = lanes([jnp.concatenate([hidden(2 * q + 1), hidden(2 * q + 2)], axis=0) for q in cells])
    size = both.shape[0] // 2
    upper = mm_nt(both, lanes([shifts(q + 1) for q in cells]))
    return upper, mm_nt(both[:size], lanes([shifts(q) for q in cells]))


def store_level(hidden_ref, grad_ref, at, hidden, grad, ch1):
    size = COLUMNS * ch1
    hidden_ref[at * size : at * size + 3 * ch1, :] = hidden.astype(BF16)
    hidden_ref[at * size + 3 * ch1 : (at + 1) * size, :] = jnp.ones((ch1, hidden.shape[1]), BF16)
    grad_ref[at * size : (at + 1) * size, :] = grad.astype(BF16)


def inner_kernel(
    place_ref,
    mid_ref,
    shifts_ref,
    right_ref,
    odd_ref,
    even_ref,
    w1_ref,
    wide_ref,
    hidden_ref,
    grad_ref,
    slope_ref,
    first_ref,
    second_ref,
    raw_ref,
    moved_ref,
):
    depth_z = mid_ref.shape[0]
    size = w1_ref.shape[0] // 3
    ch1 = size // COLUMNS
    levels = list(range(1, depth_z - 1))
    six = 6 * ch1
    three = shifts_ref.shape[0] // (depth_z // 2)
    spread_columns(shifts_ref, right_ref, wide_ref, depth_z // 2)
    raw_levels(wide_ref, odd_ref, even_ref, raw_ref, depth_z // 2)

    def store(z, hidden, grad, slope):
        store_level(hidden_ref, grad_ref, z - 1, hidden, grad, ch1)
        slope_ref[(z - 1) * ch1 : z * ch1, :] = slope[:ch1]
        moved_ref[(z - 1) * six : z * six, :] = side_by_side(grad, ch1)

    def plane(z):
        return mid_ref[z]

    def raw(z):
        return raw_ref[(z - 1) * size : z * size, :]

    def moved(z):
        return moved_ref[(z - 1) * six : z * six, :]

    def hidden(z):
        return hidden_ref[(z - 1) * size : z * size, :]

    def shifts(q):
        return shifts_ref[q * three : (q + 1) * three, :]

    pairs = [levels[k : k + 2] for k in range(0, len(levels), 2)]
    activate(pairs, plane, raw, place_ref, w1_ref, depth_z, store)
    total = None
    for pair in pairs:
        term = first_terms(pair, plane, moved)
        total = term if total is None else total + term
    first_ref[...] = total
    upper = lower = None
    cells = list(range(depth_z // 2 - 1))
    for k in range(0, len(cells), 2):
        add_upper, add_lower = second_terms(cells[k : k + 2], hidden, shifts)
        upper = add_upper if upper is None else upper + add_upper
        lower = add_lower if lower is None else lower + add_lower
    second_ref[: 2 * size, :] = upper
    second_ref[2 * size :, :] = lower


def edge_kernel(
    place_ref,
    mid_ref,
    high_ref,
    wide_ref,
    odd_ref,
    even_ref,
    shifts_ref,
    w1_ref,
    first_ref,
    second_ref,
    hidden_ref,
    grad_ref,
    slope_ref,
    sums_ref,
    begin_ref,
    moved_ref,
    fold_ref,
):
    depth_z, rows, depth_y = mid_ref.shape
    size = w1_ref.shape[0] // 3
    ch1 = size // COLUMNS
    cells = depth_z // 2
    spread_rows = wide_ref.shape[0] // cells
    ch2 = spread_rows // 3
    end = wide_ref[(cells - 1) * spread_rows :, :]
    right = even_plane(high_ref[2 * rows + ch2 :, :].astype(F32)).astype(BF16)
    above = jnp.concatenate([jnp.zeros((ch2, depth_y), BF16), high_ref[2 * rows : 2 * rows + ch2, :], right], axis=0)
    even = mm(even_ref[...], lanes([wide_ref[:spread_rows, :], above]))
    raws = {
        0: unspread(even[:, :depth_y]),
        depth_z - 1: unspread(mm(odd_ref[...], jnp.concatenate([end, above], axis=0))),
        depth_z: unspread(even[:, depth_y:]),
    }
    places = {depth_z - 1: 0, depth_z: 1, 0: 2}
    six = 6 * ch1

    def plane(z):
        if z < 0:
            return jnp.zeros((rows, depth_y), BF16)
        if z >= depth_z:
            return high_ref[(z - depth_z) * rows : (z - depth_z + 1) * rows, :]
        return mid_ref[z]

    def store(z, hidden, grad, slope):
        at = places[z]
        if z > 0:
            store_level(hidden_ref, grad_ref, at, hidden, grad, ch1)
            slope_ref[at * ch1 : (at + 1) * ch1, :] = slope[:ch1]
        else:
            begin_ref[: 3 * ch1, :] = hidden.astype(BF16)
            begin_ref[3 * ch1 :, :] = jnp.ones((ch1, depth_y), BF16)
        moved_ref[at * six : (at + 1) * six, :] = side_by_side(grad, ch1)

    def moved(z):
        return moved_ref[places[z] * six : (places[z] + 1) * six, :]

    def hidden(z):
        return hidden_ref[places[z] * size : (places[z] + 1) * size, :]

    def shifts(q):
        if q < cells:
            return shifts_ref[q * spread_rows : (q + 1) * spread_rows, :]
        return moved_three(above[ch2 : 2 * ch2].astype(F32))

    groups = [[depth_z - 1, depth_z], [0]]
    activate(groups, plane, lambda z: raws[z], place_ref, w1_ref, depth_z, store)
    at_bottom = jnp.where(place_ref[0] != 0, 1.0, 0.0)
    first = first_ref[...] + first_terms([depth_z - 1, depth_z], plane, moved)
    first = first + at_bottom * first_terms([0], plane, moved)
    upper, lower = second_terms([cells - 1], hidden, shifts)
    bottom = at_bottom * mm_nt(begin_ref[...], shifts(0))
    second = second_ref[...] + jnp.concatenate([upper[:size], upper[size:] + bottom, lower], axis=0)
    three = 3 * ch1
    wide = 3 * ch2
    main = 7 * ch1
    for a in range(2):
        sums_ref[a * three : (a + 1) * three, :wide] = second[a * size : a * size + three]
    sums_ref[2 * three : main, :wide] = second[2 * size : 2 * size + ch1]
    rest = second[2 * size + ch1 : 2 * size + three]
    sums_ref[6 * ch1 : main, wide:] = jnp.zeros((ch1, 128 - wide), F32)
    sums_ref[main : main + ch1, :] = jnp.zeros((ch1, 128), F32)
    for c in range(3):
        sums_ref[c * 2 * ch1 : (c + 1) * 2 * ch1, wide:] = rest[:, c * ch2 : (c + 1) * ch2]
    count = first.shape[0]
    fold_ref[...] = first[:, :three] + pltpu.roll(first, count - 1, 0)[:, three:]
    groups = count // WINDOW
    for b in range(3):
        block = fold_ref[pl.ds(b + 1, groups, stride=WINDOW), :]
        if b < 2:
            sums_ref[main : main + groups, b * three : (b + 1) * three] = block
        else:
            sums_ref[main : main + groups, wide : wide + ch1] = block[:, :ch1]
            sums_ref[main : main + groups, wide + ch1 :] = block[:, ch1 : 2 * ch1]
            sums_ref[6 * ch1 : 6 * ch1 + groups, wide : wide + ch1] = block[:, 2 * ch1 :]
    at = count // 3 + WINDOW - 2
    sums_ref[main + groups : main + groups + 1, :ch1] = fold_ref[at : at + 1, ch1 : 2 * ch1]
    at = size + three
    sums_ref[main + groups + 1 : main + groups + 2, :ch2] = second[at : at + 1, ch2 : 2 * ch2]


def inner(place, mid, shifts, right, odd, even, w1):
    depth_z, rows, depth_y = mid.shape
    size = w1.shape[0] // 3
    ch1 = size // COLUMNS
    ch2 = shifts.shape[0] // (3 * (depth_z // 2))
    vmem = pl.BlockSpec(memory_space=pltpu.VMEM)
    count = depth_z - 2
    return pl.pallas_call(
        inner_kernel,
        in_specs=[pl.BlockSpec(memory_space=pltpu.SMEM)] + [vmem] * 6,
        out_specs=(vmem,) * 6,
        out_shape=(
            jax.ShapeDtypeStruct(shifts.shape, BF16),
            jax.ShapeDtypeStruct((count * size, depth_y), BF16),
            jax.ShapeDtypeStruct((count * size, depth_y), BF16),
            jax.ShapeDtypeStruct((count * ch1, depth_y), F32),
            jax.ShapeDtypeStruct((3 * rows, 6 * ch1), F32),
            jax.ShapeDtypeStruct((3 * size, 3 * ch2), F32),
        ),
        scratch_shapes=[pltpu.VMEM((count * size, depth_y), F32), pltpu.VMEM((count * 6 * ch1, depth_y), BF16)],
        compiler_params=pltpu.CompilerParams(vmem_limit_bytes=VMEM_LIMIT),
        cost_estimate=pl.CostEstimate(flops=0, bytes_accessed=0, transcendentals=0),
        name="inner_levels",
    )(place, mid, shifts, right, odd, even, w1)


def edge(place, mid, high, wide, odd, even, shifts, w1, first, second):
    _, rows, depth_y = mid.shape
    size = w1.shape[0] // 3
    ch1 = size // COLUMNS
    vmem = pl.BlockSpec(memory_space=pltpu.VMEM)
    return pl.pallas_call(
        edge_kernel,
        in_specs=[pl.BlockSpec(memory_space=pltpu.SMEM)] + [vmem] * 9,
        out_specs=(vmem,) * 4,
        out_shape=(
            jax.ShapeDtypeStruct((2 * size, depth_y), BF16),
            jax.ShapeDtypeStruct((2 * size, depth_y), BF16),
            jax.ShapeDtypeStruct((2 * ch1, depth_y), F32),
            jax.ShapeDtypeStruct((8 * ch1, 128), F32),
        ),
        scratch_shapes=[
            pltpu.VMEM((size, depth_y), BF16),
            pltpu.VMEM((3 * 6 * ch1, depth_y), BF16),
            pltpu.VMEM((3 * rows, 3 * ch1), F32),
        ],
        compiler_params=pltpu.CompilerParams(vmem_limit_bytes=VMEM_LIMIT),
        name="edge_levels_and_sums",
    )(place, mid, high, wide, odd, even, shifts, w1, first, second)


def last_kernel(
    place_ref,
    low_ref,
    mid_ref,
    high_ref,
    left_ref,
    corner_ref,
    wide_ref,
    w1_ref,
    odd_ref,
    even_ref,
    hidden_ref,
    grad_ref,
    slope_ref,
    hidden_edge_ref,
    grad_edge_ref,
    slope_edge_ref,
    w2_ref,
    w4_ref,
    feat_ref,
    gin_ref,
    leftw_ref,
    hidden_low_ref,
    grad_low_ref,
    fixed_ref,
    featw_ref,
    ginw_ref,
):
    ch2, depth_q, half_y = feat_ref.shape
    c_in, _, depth_y = gin_ref.shape
    depth_z, rows, _ = mid_ref.shape
    size = hidden_edge_ref.shape[0] // 2
    ch1 = size // COLUMNS
    spread_rows = 3 * ch2

    def spread(q, count):
        left = leftw_ref[(q + 1) * ch2 : (q + 2) * ch2, :]
        if q < 0:
            rest = low_ref[2 * rows + ch2 : 2 * rows + count * ch2, :]
        elif q >= depth_q:
            rest = high_ref[2 * rows : 2 * rows + ch2, :]
        else:
            rest = wide_ref[q * spread_rows + ch2 : q * spread_rows + count * ch2, :]
        return jnp.concatenate([left, rest], axis=0)

    def plane(z):
        return low_ref[(z + 2) * rows : (z + 3) * rows, :] if z < 0 else mid_ref[z]

    leftw_ref[:ch2, :] = odd_plane(low_ref[2 * rows : 2 * rows + ch2, :].astype(F32)).astype(BF16)
    for k in range(depth_q // 2):
        pair = left_ref[k * ch2 : (k + 1) * ch2, :].astype(F32)
        at = (2 * k + 1) * ch2
        leftw_ref[at : at + ch2, :] = even_plane(pair).astype(BF16)
        leftw_ref[at + ch2 : at + 2 * ch2, :] = odd_plane(pair).astype(BF16)
    leftw_ref[(depth_q + 1) * ch2 :, :] = even_plane(corner_ref[...].astype(F32)).astype(BF16)
    below, here = spread(-1, 3), spread(0, 3)
    raws = {
        -1: unspread(mm(odd_ref[...], jnp.concatenate([below, here], axis=0))),
        0: unspread(mm(even_ref[...], here)),
    }

    def store(z, hidden, grad, slope):
        store_level(hidden_low_ref, grad_low_ref, z + 1, hidden, grad, ch1)

    activate([[-1, 0]], plane, lambda z: raws[z], place_ref, w1_ref, depth_z, store)

    two = 2 * ch2
    odd = jnp.concatenate([odd_ref[c * size : c * size + ch1, :] for c in range(3)], axis=0)
    odd = jnp.concatenate([odd[:, :two], odd[:, spread_rows : spread_rows + two]], axis=1)
    even = jnp.concatenate([even_ref[c * size : c * size + ch1, :] for c in range(3)], axis=0)[:, :two]

    def fix(z, raw):
        if z < depth_z - 1:
            slope = slope_ref[(z - 1) * ch1 : z * ch1, :]
        else:
            slope = slope_edge_ref[(z - depth_z + 1) * ch1 : (z - depth_z + 2) * ch1, :]
        fixed_ref[(z - 1) * ch1 : z * ch1, :] = (raw * slope).astype(BF16)

    for q in range(0, depth_q, 2):
        cells = [spread(k, 2) for k in (q, q + 1, q + 2)]
        pairs = lanes([jnp.concatenate(cells[n : n + 2], axis=0) for n in range(2)])
        odds, evens = mm(odd, pairs), mm(even, lanes(cells[1:]))
        for n in range(2):
            at = slice(n * depth_y, (n + 1) * depth_y)
            fix(2 * (q + n) + 1, unspread(odds[:, at]))
            fix(2 * (q + n) + 2, unspread(evens[:, at]))

    def hidden(z):
        if z < 1:
            return hidden_low_ref[(z + 1) * size : (z + 2) * size, :]
        if z < depth_z - 1:
            return hidden_ref[(z - 1) * size : z * size, :]
        return hidden_edge_ref[(z - depth_z + 1) * size : (z - depth_z + 2) * size, :]

    def grad(z):
        if z < 1:
            return grad_low_ref[(z + 1) * size : (z + 2) * size, :]
        if z < depth_z - 1:
            rest = grad_ref[(z - 1) * size + ch1 : z * size, :]
        else:
            rest = grad_edge_ref[(z - depth_z + 1) * size + ch1 : (z - depth_z + 2) * size, :]
        return jnp.concatenate([fixed_ref[(z - 1) * ch1 : z * ch1, :], rest], axis=0)

    def window(level, z):
        return jnp.concatenate([level(z + a) for a in (-1, 0, 1)], axis=0)

    pick = (
        lax.broadcasted_iota(jnp.int32, (depth_y, half_y), 0)
        == 2 * lax.broadcasted_iota(jnp.int32, (depth_y, half_y), 1)
    ).astype(F32).astype(BF16)

    for q in range(0, depth_q, 2):
        source = lanes([window(hidden, 2 * k) for k in (q, q + 1)])
        products = mm(w2_ref[...], source)
        for n in range(2):
            terms = products[:, n * depth_y : (n + 1) * depth_y]
            full = from_left(terms[:ch2]) + terms[ch2 : 2 * ch2] + from_right(terms[2 * ch2 :])
            featw_ref[pl.ds(q + n, ch2, stride=depth_q), :] = mm(full.astype(BF16), pick)
    feat_ref[...] = featw_ref[...].reshape(feat_ref.shape).astype(BF16)

    two = 2 * c_in
    for z in range(0, depth_z, 2):
        source = lanes([window(grad, k) for k in (z, z + 1)])
        products = mm(w4_ref[...], source)
        for n in range(2):
            terms = products[:, n * depth_y : (n + 1) * depth_y]
            full = from_right(terms[:two]) + terms[two : 2 * two] + from_left(terms[2 * two :])
            for x in range(2):
                at = pl.ds(2 * (z + n) + x, c_in, stride=2 * depth_z)
                ginw_ref[at, :] = full[x * c_in : (x + 1) * c_in]
    gin_ref[...] = ginw_ref[...].reshape(gin_ref.shape).astype(BF16)


def last(place, low, mid, high, left, corner, wide, w1, odd, even, inner_values, edge_values, w2, w4):
    depth_z, _, depth_y = mid.shape
    ch2, c_in = w2.shape[0] // 3, w4.shape[0] // 6
    size = w1.shape[0] // 3
    ch1 = size // COLUMNS
    depth_q = depth_z // 2
    vmem = pl.BlockSpec(memory_space=pltpu.VMEM)
    return pl.pallas_call(
        last_kernel,
        in_specs=[pl.BlockSpec(memory_space=pltpu.SMEM)] + [vmem] * 17,
        out_specs=(vmem, vmem),
        out_shape=(
            jax.ShapeDtypeStruct((ch2, depth_q, depth_y // 2), BF16),
            jax.ShapeDtypeStruct((c_in, 2 * depth_z, depth_y), BF16),
        ),
        scratch_shapes=[
            pltpu.VMEM(((depth_q + 2) * ch2, depth_y), BF16),
            pltpu.VMEM((2 * size, depth_y), BF16),
            pltpu.VMEM((2 * size, depth_y), BF16),
            pltpu.VMEM((depth_z * ch1, depth_y), BF16),
            pltpu.VMEM((ch2 * depth_q, depth_y // 2), F32),
            pltpu.VMEM((c_in * 2 * depth_z, depth_y), F32),
        ],
        compiler_params=pltpu.CompilerParams(vmem_limit_bytes=VMEM_LIMIT),
        cost_estimate=pl.CostEstimate(flops=800_000_000, bytes_accessed=10_000_000, transcendentals=0),
        name="features_and_input_grad",
    )(place, low, mid, high, left, corner, wide, w1, odd, even, *inner_values, *edge_values, w2, w4)


def unpack_kernel(sums_ref, first_ref, second_ref, bias1_ref, bias2_ref, *, scale):
    _, c_in, ch1 = first_ref.shape
    ch2 = second_ref.shape[2]
    three, wide, main = 3 * ch1, 3 * ch2, 7 * ch1
    for a in range(3):
        for b in range(3):
            for c in range(3):
                k = 9 * a + 3 * b + c
                at = a * three + b * ch1
                if at < main:
                    block = sums_ref[at : at + ch1, c * ch2 : (c + 1) * ch2]
                else:
                    at = c * 2 * ch1 + at - main
                    block = sums_ref[at : at + ch1, wide:]
                second_ref[k] = block * scale
                down, right = (main, b * three + c * ch1) if b < 2 or c < 2 else (6 * ch1, wide)
                first_ref[k] = sums_ref[down + a * c_in : down + (a + 1) * c_in, right : right + ch1] * scale
    at = main + 3 * c_in
    bias1_ref[...] = sums_ref[at : at + 1, :ch1] * scale
    bias2_ref[...] = sums_ref[at + 1 : at + 2, :ch2] * scale


def unpack(sums, scale, c_in, ch1, ch2):
    first, bias1, second, bias2 = (
        jax.ShapeDtypeStruct(shape, F32) for shape in ((27, c_in, ch1), (1, ch1), (27, ch1, ch2), (1, ch2))
    )
    first, second, bias1, bias2 = pl.pallas_call(
        functools.partial(unpack_kernel, scale=scale),
        in_specs=[pl.BlockSpec(memory_space=pltpu.VMEM)],
        out_shape=(first, second, bias1, bias2),
        compiler_params=pltpu.CompilerParams(vmem_limit_bytes=VMEM_LIMIT),
        name="unpack_sums",
    )(sums)
    first = first.reshape(3, 3, 3, c_in, ch1).transpose(4, 3, 0, 1, 2)
    second = second.reshape(3, 3, 3, ch1, ch2).transpose(4, 3, 0, 1, 2)
    return first, bias1[0], second, bias2[0]


def exchange(value, axis):
    return lax.all_to_all(value, axis, 0, 0, tiled=True)


def copies(value, count):
    return jnp.broadcast_to(value[None], (count,) + value.shape)


def shards(loaded_planes, first_kernel, first_bias, second_kernel, second_bias, cotangent):
    channels, _, planes_dev, _, width, depth_y = loaded_planes.shape
    tiles = lax.axis_size("xy")
    slabs = lax.axis_size("gz")
    ch1, ch2 = first_kernel.shape[0], second_kernel.shape[0]
    depth_z = planes_dev * tiles
    k1 = first_kernel.transpose(2, 3, 4, 1, 0).reshape(27, channels, ch1)
    k2 = second_kernel.transpose(2, 3, 4, 1, 0).reshape(27, ch1, ch2)
    g, t = lax.axis_index("gz"), lax.axis_index("xy")
    place = jnp.stack([g == 0, g == slabs - 1, t == 0, t == tiles - 1]).astype(jnp.int32)

    windows = pack(loaded_planes.reshape(channels, width, depth_y), tiles)
    mid = lax.all_to_all(windows, "xy", split_axis=0, concat_axis=0, tiled=True)

    cot = cotangent.reshape(ch2, depth_z // 2, depth_y // 2)
    shifts, pairs, w1, odd, even, w2, w4 = prepare_own(cot, k1, first_bias[None], k2, second_bias[None])
    left, right = shifted(pairs, "xy", 1), shifted(pairs, "xy", -1)
    mid, right = lax.optimization_barrier((mid, right))

    rows = mid.shape[1]
    downward = jnp.concatenate([mid[:2].reshape(2 * rows, depth_y), shifts[ch2 : 2 * ch2], right[:ch2]], axis=0)
    high = shifted(downward, "gz", -1)
    wide, *inner_values, first, second = inner(place, mid, shifts, right, odd, even, w1)
    high, left = lax.optimization_barrier((high, left))
    *edge_values, sums = edge(place, mid, high, wide, odd, even, shifts, w1, first, second)

    upward = [mid[-2:].reshape(2 * rows, depth_y), left[-ch2:], wide[-2 * ch2 :]]
    upward, corner = jnp.concatenate(upward, axis=0), left[:ch2]
    sums, upward, corner = lax.optimization_barrier((sums, upward, corner))
    part = exchange(sums.reshape(slabs, -1, sums.shape[1]), "gz").sum(0)
    part, upward, corner = lax.optimization_barrier((part, upward, corner))
    low, corner = shifted(upward, "gz", 1), shifted(corner, "gz", -1)
    part = exchange(copies(part, tiles), "xy").sum(0)
    part, low, corner = lax.optimization_barrier((part, low, corner))
    sums = exchange(copies(part, slabs), "gz").reshape(sums.shape)
    features, input_grad = last(
        place, low, mid, high, left, corner, wide, w1, odd, even, inner_values, edge_values, w2, w4
    )
    scale = 1.0 / math.sqrt(slabs * depth_z * width * depth_y)
    first_grad, first_bias_grad, second_grad, second_bias_grad = unpack(sums, scale, channels, ch1, ch2)
    return (
        features[:, :, None, :],
        input_grad.reshape(channels, depth_z, 2, depth_y),
        first_grad,
        first_bias_grad,
        second_grad,
        second_bias_grad,
    )


def solution(mesh):
    return jax.shard_map(
        shards,
        mesh=mesh,
        in_specs=(
            P(None, "gz", None, "xy", None, None),
            P(),
            P(),
            P(),
            P(),
            P(None, "gz", "xy", None),
        ),
        out_specs=(P(None, "gz", "xy", None), P(None, "gz", "xy", None), P(), P(), P(), P()),
        check_vma=False,
    )
```

```python
import functools
import math

import jax
import jax.numpy as jnp
from jax import lax
from jax.experimental import pallas as pl
from jax.experimental.pallas import tpu as pltpu
from jax.sharding import PartitionSpec as P

BF16 = jnp.bfloat16
F32 = jnp.float32
WINDOW = 8
COLUMNS = 4
VMEM_LIMIT = 12 * 1024 * 1024


def shifted(value, axis, steps):
    count = lax.axis_size(axis)
    first, last = (max(0, -steps), min(count, count - steps))
    return lax.ppermute(value, axis, [(source, source + steps) for source in range(first, last)])


def mm(left, right):
    return jnp.dot(left, right, preferred_element_type=F32)


def mm_nt(left, right):
    return lax.dot_general(left, right, (((1,), (1,)), ((), ())), preferred_element_type=F32)


def from_left(value):
    lane = lax.broadcasted_iota(jnp.int32, value.shape, 1)
    return jnp.where(lane == 0, 0.0, pltpu.roll(value, 1, 1))


def from_right(value):
    lane = lax.broadcasted_iota(jnp.int32, value.shape, 1)
    last = value.shape[1] - 1
    return jnp.where(lane == last, 0.0, pltpu.roll(value, last, 1))


def lanes(blocks):
    return blocks[0] if len(blocks) == 1 else jnp.concatenate(blocks, axis=1)


def pack_kernel(planes_ref, out_ref, wide_ref):
    channels, width, _ = planes_ref.shape
    wide_ref[...] = jnp.zeros_like(wide_ref)
    wide_ref[:, 8 : 8 + width, :] = planes_ref[...].astype(F32)
    targets = out_ref.shape[0]
    row = lax.broadcasted_iota(jnp.int32, (WINDOW, out_ref.shape[2]), 0)
    for t in range(targets):
        parts = [wide_ref[i, 6 + 2 * t : 6 + 2 * t + WINDOW, :] for i in range(channels)]
        parts = [jnp.where(row >= WINDOW - 2, 1.0, part) for part in parts]
        out_ref[t] = jnp.concatenate(parts, axis=0).astype(BF16)


def pack(planes, targets):
    channels, width, depth_y = planes.shape
    shape = (targets, channels * WINDOW, depth_y)
    return pl.pallas_call(
        pack_kernel,
        out_shape=jax.ShapeDtypeStruct(shape, BF16),
        scratch_shapes=[pltpu.VMEM((channels, width + 16, depth_y), F32)],
        compiler_params=pltpu.CompilerParams(vmem_limit_bytes=VMEM_LIMIT),
        name="pack_windows",
    )(planes)


def split_bias(bias):
    high = bias.astype(BF16).astype(F32)
    middle = (bias - high).astype(BF16).astype(F32)
    return high, middle, bias - high - middle


def first_matrix(kernel_ref, bias_ref, turned_ref):
    _, c_in, ch1 = kernel_ref.shape
    size = COLUMNS * ch1
    turned_ref[...] = jnp.zeros_like(turned_ref)
    nothing = jnp.zeros((c_in, ch1), F32)

    def block(a, b, c):
        return kernel_ref[9 * a + 3 * b + c].astype(F32) if 0 <= b < 3 and c < 3 else nothing

    for a in range(3):
        for w in range(COLUMNS + 2):
            at = pl.ds(a * c_in * WINDOW + w, c_in, stride=WINDOW)
            for half in range(2):
                blocks = [block(a, w - x, c) for c in (2 * half, 2 * half + 1) for x in range(COLUMNS)]
                turned_ref[half, at, :] = jnp.concatenate(blocks, axis=1)
    for n, part in enumerate(split_bias(bias_ref[...])):
        row = c_in * WINDOW + n * WINDOW + WINDOW - 2
        for x in range(COLUMNS):
            half, right = divmod(size + x * ch1, 128)
            turned_ref[half, row : row + 1, right : right + ch1] = part
    return jnp.concatenate([turned_ref[0].T, turned_ref[1].T], axis=0)[: 3 * size].astype(BF16)


def spread_matrix(kernel_ref, out_ref, row, a, column):
    _, ch1, ch2 = kernel_ref.shape
    for c in range(3):
        for x in range(COLUMNS):
            for q in range(3):
                b = x - 1 - 2 * (q - 1) + 1
                if 0 <= b <= 2:
                    down, right = row + (c * COLUMNS + x) * ch1, column + q * ch2
                    out_ref[down : down + ch1, right : right + ch2] = kernel_ref[9 * a + 3 * b + c]


def unspread(terms):
    size = terms.shape[0] // 3
    return from_right(terms[:size]) + terms[size : 2 * size] + from_left(terms[2 * size :])


def moved_three(value):
    return jnp.concatenate([from_right(value), value, from_left(value)], axis=0).astype(BF16)


def even_plane(pair):
    lane = lax.broadcasted_iota(jnp.int32, pair.shape, 1)
    return jnp.where(lane % 2 == 0, pair, 0.0)


def odd_plane(pair):
    return even_plane(from_right(pair))


def second_matrix(kernel_ref, bias_ref, turned_ref):
    _, ch1, ch2 = kernel_ref.shape
    size = COLUMNS * ch1
    turned_ref[...] = jnp.zeros_like(turned_ref)
    for a in range(3):
        for b in range(3):
            for c in range(3):
                at = a * size + b * ch1
                turned_ref[at : at + ch1, c * ch2 : (c + 1) * ch2] = kernel_ref[9 * a + 3 * b + c].astype(F32)
    for n, part in enumerate(split_bias(bias_ref[...])):
        row = size + 3 * ch1 + n
        turned_ref[row : row + 1, ch2 : 2 * ch2] = part
    return turned_ref[...].T[: 3 * ch2].astype(BF16)


def back_matrix(kernel_ref, flat_ref):
    _, c_in, ch1 = kernel_ref.shape
    size = COLUMNS * ch1
    flat_ref[...] = jnp.zeros_like(flat_ref)
    for a in range(3):
        for b in range(3):
            for c in range(3):
                for x in range(2):
                    down, right = (c * 2 + x) * c_in, (2 - a) * size + (x + 2 - b) * ch1
                    block = kernel_ref[9 * a + 3 * b + c].astype(F32)
                    flat_ref[down : down + c_in, right : right + ch1] = block
    return flat_ref[...].astype(BF16)


def own_kernel(
    mid_ref,
    k1_ref,
    b1_ref,
    k2_ref,
    b2_ref,
    shifts_ref,
    pairs_ref,
    w1_ref,
    odd_ref,
    even_ref,
    odd_own_ref,
    even_own_ref,
    w2_ref,
    w4_ref,
    flat_ref,
    turned_ref,
    turned2_ref,
    flat4_ref,
):
    ch2, cells, half_y = mid_ref.shape
    rows = 3 * ch2
    depth_y = 2 * half_y
    spread = (
        2 * lax.broadcasted_iota(jnp.int32, (half_y, depth_y), 0)
        == lax.broadcasted_iota(jnp.int32, (half_y, depth_y), 1)
    ).astype(F32).astype(BF16)
    flat_ref[...] = mid_ref[...].astype(F32).reshape(ch2 * cells, half_y)
    for q in range(cells):
        wide = mm(flat_ref[pl.ds(q, ch2, stride=cells), :].astype(BF16), spread)
        shifts_ref[q * rows : (q + 1) * rows, :] = moved_three(wide)
        if q % 2 == 0:
            first = wide
        else:
            pairs_ref[q // 2 * ch2 : (q // 2 + 1) * ch2, :] = (first + from_left(wide)).astype(BF16)
    w1_ref[...] = first_matrix(k1_ref, b1_ref, turned_ref)
    odd_ref[...] = jnp.zeros_like(odd_ref)
    even_ref[...] = jnp.zeros_like(even_ref)
    spread_matrix(k2_ref, odd_ref, 0, 2, 0)
    spread_matrix(k2_ref, odd_ref, 0, 0, rows)
    spread_matrix(k2_ref, even_ref, 0, 1, 0)
    size = even_ref.shape[0] // 3
    ch1 = size // COLUMNS
    odd = jnp.concatenate([odd_ref[c * size + ch1 : (c + 1) * size, :] for c in range(3)], axis=0)
    odd_own_ref[...] = jnp.concatenate([odd[:, ch2:rows], odd[:, rows + ch2 :]], axis=1)
    even = jnp.concatenate([even_ref[c * size + ch1 : (c + 1) * size, :] for c in range(3)], axis=0)
    even_own_ref[...] = even[:, ch2:]
    w2_ref[...] = second_matrix(k2_ref, b2_ref, turned2_ref)
    w4_ref[...] = back_matrix(k1_ref, flat4_ref)


def prepare_own(mid, k1, b1, k2, b2):
    ch2, cells, half_y = mid.shape
    _, c_in, ch1 = k1.shape
    depth_y = 2 * half_y
    size, rows = COLUMNS * ch1, 3 * ch2
    return pl.pallas_call(
        own_kernel,
        out_shape=(
            jax.ShapeDtypeStruct((cells * rows, depth_y), BF16),
            jax.ShapeDtypeStruct((cells // 2 * ch2, depth_y), BF16),
            jax.ShapeDtypeStruct((3 * size, 3 * c_in * WINDOW), BF16),
            jax.ShapeDtypeStruct((3 * size, 2 * rows), BF16),
            jax.ShapeDtypeStruct((3 * size, rows), BF16),
            jax.ShapeDtypeStruct((3 * (size - ch1), 4 * ch2), BF16),
            jax.ShapeDtypeStruct((3 * (size - ch1), 2 * ch2), BF16),
            jax.ShapeDtypeStruct((rows, 3 * size), BF16),
            jax.ShapeDtypeStruct((6 * c_in, 3 * size), BF16),
        ),
        scratch_shapes=[
            pltpu.VMEM((ch2 * cells, half_y), F32),
            pltpu.VMEM((2, 3 * c_in * WINDOW, 128), F32),
            pltpu.VMEM((3 * size, 128), F32),
            pltpu.VMEM((6 * c_in, 3 * size), F32),
        ],
        compiler_params=pltpu.CompilerParams(vmem_limit_bytes=VMEM_LIMIT),
        cost_estimate=pl.CostEstimate(flops=100_000_000, bytes_accessed=2_000_000, transcendentals=0),
        name="spread_cotangent",
    )(mid, k1, b1, k2, b2)


def raw_levels(shifts_ref, right_ref, odd_ref, even_ref, raw_ref, wide_ref):
    ch2 = even_ref.shape[1] // 2
    cells = right_ref.shape[0] // ch2 * 2
    size = even_ref.shape[0] // 3
    rows = 2 * ch2
    depth_y = shifts_ref.shape[1]
    for q in range(cells):
        at = (3 * q + 1) * ch2
        wide_ref[q * rows : q * rows + ch2, :] = shifts_ref[at : at + ch2, :]
        pair = right_ref[q // 2 * ch2 : (q // 2 + 1) * ch2, :].astype(F32)
        plane = odd_plane(pair) if q % 2 else even_plane(pair)
        wide_ref[q * rows + ch2 : (q + 1) * rows, :] = plane.astype(BF16)

    def store(z, terms):
        raw_ref[z * size : (z + 1) * size, :] = unspread(terms)

    for m in range(0, cells, 2):
        even = mm(even_ref[...], lanes([wide_ref[k * rows : (k + 1) * rows, :] for k in (m, m + 1)]))
        group = [k for k in (m, m + 1) if k < cells - 1]
        odd = mm(odd_ref[...], lanes([wide_ref[k * rows : (k + 2) * rows, :] for k in group]))
        for n, k in enumerate((m, m + 1)):
            store(2 * k, even[:, n * depth_y : (n + 1) * depth_y])
        for n, k in enumerate(group):
            store(2 * k + 1, odd[:, n * depth_y : (n + 1) * depth_y])


def activate(groups, plane, place_ref, w1_ref, depth_z, store):
    size = w1_ref.shape[0] // 3
    ch1 = size // COLUMNS
    at_first_z, at_last_z, at_first_x, at_last_x = (place_ref[k] for k in range(4))
    depth_y = plane(groups[0][0]).shape[1]
    row = lax.broadcasted_iota(jnp.int32, (size, depth_y), 0)
    outside = ((row < ch1) & (at_first_x != 0)) | ((row >= 3 * ch1) & (at_last_x != 0))
    inside = jnp.where(outside, 0.0, 1.0)
    for group in groups:
        source = lanes([jnp.concatenate([plane(z + a) for a in (-1, 0, 1)], axis=0) for z in group])
        products = mm(w1_ref[...], source)
        for n, z in enumerate(group):
            terms = products[:, n * depth_y : (n + 1) * depth_y]
            pre = from_left(terms[:size]) + terms[size : 2 * size] + from_right(terms[2 * size :])
            sigma = 1.0 / (1.0 + jnp.exp(-pre))
            keep = inside
            if z == -1:
                keep = inside * jnp.where(at_first_z != 0, 0.0, 1.0)
            if z == depth_z:
                keep = inside * jnp.where(at_last_z != 0, 0.0, 1.0)
            kept = sigma * keep
            slope = kept * (1.0 + pre * (1.0 - sigma))
            store(z, (pre * kept)[: 3 * ch1], slope)


def side_by_side(grad, ch1):
    own = grad[: 2 * ch1]
    parts = [from_right(own), own, from_left(own)]
    sides = [part[x * ch1 : (x + 1) * ch1] for x in range(2) for part in parts]
    return jnp.concatenate(sides, axis=0).astype(BF16)


def first_terms(levels, plane, moved):
    source = lanes([jnp.concatenate([plane(z + a) for a in (-1, 0, 1)], axis=0) for z in levels])
    return mm_nt(source, lanes([moved(z) for z in levels]))


def second_terms(cells, hidden, shifts):
    both = lanes([jnp.concatenate([hidden(2 * q + 1), hidden(2 * q + 2)], axis=0) for q in cells])
    size = both.shape[0] // 2
    upper = mm_nt(both, lanes([shifts(q + 1) for q in cells]))
    return upper, mm_nt(both[:size], lanes([shifts(q) for q in cells]))


def store_level(hidden_ref, grad_ref, at, hidden, grad, ch1):
    size = COLUMNS * ch1
    hidden_ref[at * size : at * size + 3 * ch1, :] = hidden.astype(BF16)
    hidden_ref[at * size + 3 * ch1 : (at + 1) * size, :] = jnp.ones((ch1, hidden.shape[1]), BF16)
    grad_ref[at * grad.shape[0] : (at + 1) * grad.shape[0], :] = grad.astype(BF16)


def inner_kernel(
    place_ref,
    mid_ref,
    shifts_ref,
    right_ref,
    odd_ref,
    even_ref,
    w1_ref,
    hidden_ref,
    grad_ref,
    slope_ref,
    first_ref,
    second_ref,
    raw_ref,
    wide_ref,
    begin_ref,
    moved_ref,
):
    depth_z, rows, depth_y = mid_ref.shape
    size = w1_ref.shape[0] // 3
    ch1 = size // COLUMNS
    six = 6 * ch1
    known = size - ch1
    three = shifts_ref.shape[0] // (depth_z // 2)
    raw_levels(shifts_ref, right_ref, odd_ref, even_ref, raw_ref, wide_ref)

    def plane(z):
        return mid_ref[z] if z >= 0 else jnp.zeros((rows, depth_y), BF16)

    def store(z, hidden, slope):
        grad = raw_ref[z * known : (z + 1) * known, :] * slope[ch1:]
        moved_ref[z * six : (z + 1) * six, :] = side_by_side(grad, ch1)
        if z == 0:
            begin_ref[: 3 * ch1, :] = hidden.astype(BF16)
            begin_ref[3 * ch1 :, :] = jnp.ones((ch1, depth_y), BF16)
        else:
            store_level(hidden_ref, grad_ref, z - 1, hidden, grad, ch1)
            slope_ref[(z - 1) * ch1 : z * ch1, :] = slope[:ch1]

    def moved(z):
        return moved_ref[z * six : (z + 1) * six, :]

    def hidden(z):
        return hidden_ref[(z - 1) * size : z * size, :]

    def shifts(q):
        return shifts_ref[q * three : (q + 1) * three, :]

    levels = list(range(1, depth_z - 1))
    pairs = [levels[k : k + 2] for k in range(0, len(levels), 2)]
    activate([[0]] + pairs, plane, place_ref, w1_ref, depth_z, store)
    at_bottom = jnp.where(place_ref[0] != 0, 1.0, 0.0)
    total = at_bottom * first_terms([0], plane, moved)
    for pair in pairs:
        total = total + first_terms(pair, plane, moved)
    first_ref[...] = total
    upper = lower = None
    cells = list(range(depth_z // 2 - 1))
    for k in range(0, len(cells), 2):
        add_upper, add_lower = second_terms(cells[k : k + 2], hidden, shifts)
        upper = add_upper if upper is None else upper + add_upper
        lower = add_lower if lower is None else lower + add_lower
    second_ref[:size, :] = upper[:size]
    second_ref[size : 2 * size, :] = upper[size:] + at_bottom * mm_nt(begin_ref[...], shifts(0))
    second_ref[2 * size :, :] = lower


def edge_kernel(
    place_ref,
    mid_ref,
    high_ref,
    right_ref,
    odd_ref,
    even_ref,
    shifts_ref,
    w1_ref,
    first_ref,
    second_ref,
    hidden_ref,
    grad_ref,
    slope_ref,
    sums_ref,
    moved_ref,
    fold_ref,
):
    depth_z, rows, depth_y = mid_ref.shape
    size = w1_ref.shape[0] // 3
    ch1 = size // COLUMNS
    cells = depth_z // 2
    ch2 = even_ref.shape[1] // 2
    spread_rows = 3 * ch2
    own = high_ref[2 * rows : 2 * rows + ch2, :]
    beyond = even_plane(high_ref[2 * rows + ch2 :, :].astype(F32)).astype(BF16)
    above = jnp.concatenate([own, beyond], axis=0)
    at = (3 * cells - 2) * ch2
    last_right = odd_plane(right_ref[...][-ch2:].astype(F32)).astype(BF16)
    end = jnp.concatenate([shifts_ref[at : at + ch2, :], last_right], axis=0)
    raws = {
        depth_z - 1: unspread(mm(odd_ref[...], jnp.concatenate([end, above], axis=0))),
        depth_z: unspread(mm(even_ref[...], above)),
    }
    places = {depth_z - 1: 0, depth_z: 1}
    six = 6 * ch1

    def plane(z):
        if z >= depth_z:
            return high_ref[(z - depth_z) * rows : (z - depth_z + 1) * rows, :]
        return mid_ref[z]

    def store(z, hidden, slope):
        at = places[z]
        grad = raws[z] * slope[ch1:]
        store_level(hidden_ref, grad_ref, at, hidden, grad, ch1)
        slope_ref[at * ch1 : (at + 1) * ch1, :] = slope[:ch1]
        moved_ref[at * six : (at + 1) * six, :] = side_by_side(grad, ch1)

    def moved(z):
        return moved_ref[places[z] * six : (places[z] + 1) * six, :]

    def hidden(z):
        return hidden_ref[places[z] * size : (places[z] + 1) * size, :]

    def shifts(q):
        if q < cells:
            return shifts_ref[q * spread_rows : (q + 1) * spread_rows, :]
        return moved_three(own.astype(F32))

    activate([[depth_z - 1, depth_z]], plane, place_ref, w1_ref, depth_z, store)
    first = first_ref[...] + first_terms([depth_z - 1, depth_z], plane, moved)
    upper, lower = second_terms([cells - 1], hidden, shifts)
    second = second_ref[...] + jnp.concatenate([upper, lower], axis=0)
    three = 3 * ch1
    wide = 3 * ch2
    main = 7 * ch1
    for a in range(2):
        sums_ref[a * three : (a + 1) * three, :wide] = second[a * size : a * size + three]
    sums_ref[2 * three : main, :wide] = second[2 * size : 2 * size + ch1]
    rest = second[2 * size + ch1 : 2 * size + three]
    sums_ref[6 * ch1 : main, wide:] = jnp.zeros((ch1, 128 - wide), F32)
    sums_ref[main : main + ch1, :] = jnp.zeros((ch1, 128), F32)
    for c in range(3):
        sums_ref[c * 2 * ch1 : (c + 1) * 2 * ch1, wide:] = rest[:, c * ch2 : (c + 1) * ch2]
    count = first.shape[0]
    fold_ref[...] = first[:, :three] + pltpu.roll(first, count - 1, 0)[:, three:]
    groups = count // WINDOW
    for b in range(3):
        block = fold_ref[pl.ds(b + 1, groups, stride=WINDOW), :]
        if b < 2:
            sums_ref[main : main + groups, b * three : (b + 1) * three] = block
        else:
            sums_ref[main : main + groups, wide : wide + ch1] = block[:, :ch1]
            sums_ref[main : main + groups, wide + ch1 :] = block[:, ch1 : 2 * ch1]
            sums_ref[6 * ch1 : 6 * ch1 + groups, wide : wide + ch1] = block[:, 2 * ch1 :]
    at = count // 3 + WINDOW - 2
    sums_ref[main + groups : main + groups + 1, :ch1] = fold_ref[at : at + 1, ch1 : 2 * ch1]
    at = size + three
    sums_ref[main + groups + 1 : main + groups + 2, :ch2] = second[at : at + 1, ch2 : 2 * ch2]


def inner(place, mid, shifts, right, odd, even, w1):
    depth_z, rows, depth_y = mid.shape
    size = w1.shape[0] // 3
    ch1 = size // COLUMNS
    ch2 = shifts.shape[0] // (3 * (depth_z // 2))
    vmem = pl.BlockSpec(memory_space=pltpu.VMEM)
    count = depth_z - 2
    return pl.pallas_call(
        inner_kernel,
        in_specs=[pl.BlockSpec(memory_space=pltpu.SMEM)] + [vmem] * 6,
        out_specs=(vmem,) * 5,
        out_shape=(
            jax.ShapeDtypeStruct((count * size, depth_y), BF16),
            jax.ShapeDtypeStruct((count * (size - ch1), depth_y), BF16),
            jax.ShapeDtypeStruct((count * ch1, depth_y), F32),
            jax.ShapeDtypeStruct((3 * rows, 6 * ch1), F32),
            jax.ShapeDtypeStruct((3 * size, 3 * ch2), F32),
        ),
        scratch_shapes=[
            pltpu.VMEM(((count + 1) * (size - ch1), depth_y), F32),
            pltpu.VMEM((depth_z * ch2, depth_y), BF16),
            pltpu.VMEM((size, depth_y), BF16),
            pltpu.VMEM(((count + 1) * 6 * ch1, depth_y), BF16),
        ],
        compiler_params=pltpu.CompilerParams(vmem_limit_bytes=VMEM_LIMIT),
        cost_estimate=pl.CostEstimate(flops=0, bytes_accessed=0, transcendentals=0),
        name="inner_levels",
    )(place, mid, shifts, right, odd, even, w1)


def edge(place, mid, high, right, odd, even, shifts, w1, first, second):
    _, rows, depth_y = mid.shape
    size = w1.shape[0] // 3
    ch1 = size // COLUMNS
    vmem = pl.BlockSpec(memory_space=pltpu.VMEM)
    return pl.pallas_call(
        edge_kernel,
        in_specs=[pl.BlockSpec(memory_space=pltpu.SMEM)] + [vmem] * 9,
        out_specs=(vmem,) * 4,
        out_shape=(
            jax.ShapeDtypeStruct((2 * size, depth_y), BF16),
            jax.ShapeDtypeStruct((2 * (size - ch1), depth_y), BF16),
            jax.ShapeDtypeStruct((2 * ch1, depth_y), F32),
            jax.ShapeDtypeStruct((8 * ch1, 128), F32),
        ),
        scratch_shapes=[
            pltpu.VMEM((2 * 6 * ch1, depth_y), BF16),
            pltpu.VMEM((3 * rows, 3 * ch1), F32),
        ],
        compiler_params=pltpu.CompilerParams(vmem_limit_bytes=VMEM_LIMIT),
        name="edge_levels_and_sums",
    )(place, mid, high, right, odd, even, shifts, w1, first, second)


def last_kernel(
    place_ref,
    low_ref,
    mid_ref,
    high_ref,
    left_ref,
    corner_ref,
    right_ref,
    shifts_ref,
    w1_ref,
    odd_ref,
    even_ref,
    hidden_ref,
    grad_ref,
    slope_ref,
    hidden_edge_ref,
    grad_edge_ref,
    slope_edge_ref,
    w2_ref,
    w4_ref,
    feat_ref,
    gin_ref,
    leftw_ref,
    hidden_low_ref,
    grad_low_ref,
    fixed_ref,
    featw_ref,
    ginw_ref,
):
    ch2, depth_q, half_y = feat_ref.shape
    c_in, _, depth_y = gin_ref.shape
    depth_z, rows, _ = mid_ref.shape
    size = hidden_edge_ref.shape[0] // 2
    ch1 = size // COLUMNS
    spread_rows = 3 * ch2

    def spread(q):
        left = leftw_ref[(q + 1) * ch2 : (q + 2) * ch2, :]
        if q < 0:
            own = low_ref[2 * rows + ch2 : 2 * rows + 2 * ch2, :]
        elif q >= depth_q:
            own = high_ref[2 * rows : 2 * rows + ch2, :]
        else:
            own = shifts_ref[(3 * q + 1) * ch2 : (3 * q + 2) * ch2, :]
        return jnp.concatenate([left, own], axis=0)

    def plane(z):
        return low_ref[(z + 2) * rows : (z + 3) * rows, :] if z < 0 else mid_ref[z]

    leftw_ref[:ch2, :] = odd_plane(low_ref[2 * rows : 2 * rows + ch2, :].astype(F32)).astype(BF16)
    for k in range(depth_q // 2):
        pair = left_ref[k * ch2 : (k + 1) * ch2, :].astype(F32)
        at = (2 * k + 1) * ch2
        leftw_ref[at : at + ch2, :] = even_plane(pair).astype(BF16)
        leftw_ref[at + ch2 : at + 2 * ch2, :] = odd_plane(pair).astype(BF16)
    leftw_ref[(depth_q + 1) * ch2 :, :] = even_plane(corner_ref[...].astype(F32)).astype(BF16)
    below = odd_plane(low_ref[2 * rows + 2 * ch2 :, :].astype(F32)).astype(BF16)
    here = even_plane(right_ref[:ch2, :].astype(F32)).astype(BF16)
    below, here = (jnp.concatenate([spread(q), side], axis=0) for q, side in ((-1, below), (0, here)))
    raws = {
        -1: unspread(mm(odd_ref[...], jnp.concatenate([below, here], axis=0))),
        0: unspread(mm(even_ref[...], here)),
    }

    def store(z, hidden, slope):
        store_level(hidden_low_ref, grad_low_ref, z + 1, hidden, raws[z] * slope, ch1)

    activate([[-1, 0]], plane, place_ref, w1_ref, depth_z, store)

    two = 2 * ch2
    odd = jnp.concatenate([odd_ref[c * size : c * size + ch1, :] for c in range(3)], axis=0)
    odd = jnp.concatenate([odd[:, :two], odd[:, spread_rows : spread_rows + two]], axis=1)
    even = jnp.concatenate([even_ref[c * size : c * size + ch1, :] for c in range(3)], axis=0)[:, :two]

    def fix(z, raw):
        if z < depth_z - 1:
            slope = slope_ref[(z - 1) * ch1 : z * ch1, :]
        else:
            slope = slope_edge_ref[(z - depth_z + 1) * ch1 : (z - depth_z + 2) * ch1, :]
        fixed_ref[(z - 1) * ch1 : z * ch1, :] = (raw * slope).astype(BF16)

    for q in range(0, depth_q, 2):
        cells = [spread(k) for k in (q, q + 1, q + 2)]
        pairs = lanes([jnp.concatenate(cells[n : n + 2], axis=0) for n in range(2)])
        odds, evens = mm(odd, pairs), mm(even, lanes(cells[1:]))
        for n in range(2):
            at = slice(n * depth_y, (n + 1) * depth_y)
            fix(2 * (q + n) + 1, unspread(odds[:, at]))
            fix(2 * (q + n) + 2, unspread(evens[:, at]))

    def hidden(z):
        if z < 1:
            return hidden_low_ref[(z + 1) * size : (z + 2) * size, :]
        if z < depth_z - 1:
            return hidden_ref[(z - 1) * size : z * size, :]
        return hidden_edge_ref[(z - depth_z + 1) * size : (z - depth_z + 2) * size, :]

    known = size - ch1

    def grad(z):
        if z < 1:
            return grad_low_ref[(z + 1) * size : (z + 2) * size, :]
        if z < depth_z - 1:
            rest = grad_ref[(z - 1) * known : z * known, :]
        else:
            rest = grad_edge_ref[(z - depth_z + 1) * known : (z - depth_z + 2) * known, :]
        return jnp.concatenate([fixed_ref[(z - 1) * ch1 : z * ch1, :], rest], axis=0)

    def window(level, z):
        return jnp.concatenate([level(z + a) for a in (-1, 0, 1)], axis=0)

    pick = (
        lax.broadcasted_iota(jnp.int32, (depth_y, half_y), 0)
        == 2 * lax.broadcasted_iota(jnp.int32, (depth_y, half_y), 1)
    ).astype(F32).astype(BF16)

    for q in range(0, depth_q, 2):
        source = lanes([window(hidden, 2 * k) for k in (q, q + 1)])
        products = mm(w2_ref[...], source)
        for n in range(2):
            terms = products[:, n * depth_y : (n + 1) * depth_y]
            full = from_left(terms[:ch2]) + terms[ch2 : 2 * ch2] + from_right(terms[2 * ch2 :])
            featw_ref[pl.ds(q + n, ch2, stride=depth_q), :] = mm(full.astype(BF16), pick)
    feat_ref[...] = featw_ref[...].reshape(feat_ref.shape).astype(BF16)

    two = 2 * c_in
    for z in range(0, depth_z, 2):
        source = lanes([window(grad, k) for k in (z, z + 1)])
        products = mm(w4_ref[...], source)
        for n in range(2):
            terms = products[:, n * depth_y : (n + 1) * depth_y]
            full = from_right(terms[:two]) + terms[two : 2 * two] + from_left(terms[2 * two :])
            for x in range(2):
                at = pl.ds(2 * (z + n) + x, c_in, stride=2 * depth_z)
                ginw_ref[at, :] = full[x * c_in : (x + 1) * c_in]
    gin_ref[...] = ginw_ref[...].reshape(gin_ref.shape).astype(BF16)


def last(place, low, mid, high, left, corner, right, shifts, w1, odd, even, inner_values, edge_values, w2, w4):
    depth_z, _, depth_y = mid.shape
    ch2, c_in = w2.shape[0] // 3, w4.shape[0] // 6
    size = w1.shape[0] // 3
    ch1 = size // COLUMNS
    depth_q = depth_z // 2
    vmem = pl.BlockSpec(memory_space=pltpu.VMEM)
    return pl.pallas_call(
        last_kernel,
        in_specs=[pl.BlockSpec(memory_space=pltpu.SMEM)] + [vmem] * 18,
        out_specs=(vmem, vmem),
        out_shape=(
            jax.ShapeDtypeStruct((ch2, depth_q, depth_y // 2), BF16),
            jax.ShapeDtypeStruct((c_in, 2 * depth_z, depth_y), BF16),
        ),
        scratch_shapes=[
            pltpu.VMEM(((depth_q + 2) * ch2, depth_y), BF16),
            pltpu.VMEM((2 * size, depth_y), BF16),
            pltpu.VMEM((2 * size, depth_y), BF16),
            pltpu.VMEM((depth_z * ch1, depth_y), BF16),
            pltpu.VMEM((ch2 * depth_q, depth_y // 2), F32),
            pltpu.VMEM((c_in * 2 * depth_z, depth_y), F32),
        ],
        compiler_params=pltpu.CompilerParams(vmem_limit_bytes=VMEM_LIMIT),
        cost_estimate=pl.CostEstimate(flops=800_000_000, bytes_accessed=10_000_000, transcendentals=0),
        name="features_and_input_grad",
    )(place, low, mid, high, left, corner, right, shifts, w1, odd, even, *inner_values, *edge_values, w2, w4)


def unpack_kernel(sums_ref, first_ref, second_ref, bias1_ref, bias2_ref, *, scale):
    _, c_in, ch1 = first_ref.shape
    ch2 = second_ref.shape[2]
    three, wide, main = 3 * ch1, 3 * ch2, 7 * ch1
    for a in range(3):
        for b in range(3):
            for c in range(3):
                k = 9 * a + 3 * b + c
                at = a * three + b * ch1
                if at < main:
                    block = sums_ref[at : at + ch1, c * ch2 : (c + 1) * ch2]
                else:
                    at = c * 2 * ch1 + at - main
                    block = sums_ref[at : at + ch1, wide:]
                second_ref[k] = block * scale
                down, right = (main, b * three + c * ch1) if b < 2 or c < 2 else (6 * ch1, wide)
                first_ref[k] = sums_ref[down + a * c_in : down + (a + 1) * c_in, right : right + ch1] * scale
    at = main + 3 * c_in
    bias1_ref[...] = sums_ref[at : at + 1, :ch1] * scale
    bias2_ref[...] = sums_ref[at + 1 : at + 2, :ch2] * scale


def unpack(sums, scale, c_in, ch1, ch2):
    first, bias1, second, bias2 = (
        jax.ShapeDtypeStruct(shape, F32) for shape in ((27, c_in, ch1), (1, ch1), (27, ch1, ch2), (1, ch2))
    )
    first, second, bias1, bias2 = pl.pallas_call(
        functools.partial(unpack_kernel, scale=scale),
        in_specs=[pl.BlockSpec(memory_space=pltpu.VMEM)],
        out_shape=(first, second, bias1, bias2),
        compiler_params=pltpu.CompilerParams(vmem_limit_bytes=VMEM_LIMIT),
        name="unpack_sums",
    )(sums)
    first = first.reshape(3, 3, 3, c_in, ch1).transpose(4, 3, 0, 1, 2)
    second = second.reshape(3, 3, 3, ch1, ch2).transpose(4, 3, 0, 1, 2)
    return first, bias1[0], second, bias2[0]


def exchange(value, axis):
    return lax.all_to_all(value, axis, 0, 0, tiled=True)


def copies(value, count):
    return jnp.broadcast_to(value[None], (count,) + value.shape)


def shards(loaded_planes, first_kernel, first_bias, second_kernel, second_bias, cotangent):
    channels, _, planes_dev, _, width, depth_y = loaded_planes.shape
    tiles = lax.axis_size("xy")
    slabs = lax.axis_size("gz")
    ch1, ch2 = first_kernel.shape[0], second_kernel.shape[0]
    depth_z = planes_dev * tiles
    k1 = first_kernel.transpose(2, 3, 4, 1, 0).reshape(27, channels, ch1)
    k2 = second_kernel.transpose(2, 3, 4, 1, 0).reshape(27, ch1, ch2)
    g, t = lax.axis_index("gz"), lax.axis_index("xy")
    place = jnp.stack([g == 0, g == slabs - 1, t == 0, t == tiles - 1]).astype(jnp.int32)

    windows = pack(loaded_planes.reshape(channels, width, depth_y), tiles)
    mid = lax.all_to_all(windows, "xy", split_axis=0, concat_axis=0, tiled=True)

    cot = cotangent.reshape(ch2, depth_z // 2, depth_y // 2)
    shifts, pairs, w1, odd, even, odd_own, even_own, w2, w4 = prepare_own(
        cot, k1, first_bias[None], k2, second_bias[None]
    )
    left, right = shifted(pairs, "xy", 1), shifted(pairs, "xy", -1)
    mid, right = lax.optimization_barrier((mid, right))

    rows = mid.shape[1]
    downward = jnp.concatenate([mid[:2].reshape(2 * rows, depth_y), shifts[ch2 : 2 * ch2], right[:ch2]], axis=0)
    high = shifted(downward, "gz", -1)
    *inner_values, first, second = inner(place, mid, shifts, right, odd_own, even_own, w1)
    high, left = lax.optimization_barrier((high, left))
    *edge_values, sums = edge(place, mid, high, right, odd_own, even_own, shifts, w1, first, second)

    upward = [mid[-2:].reshape(2 * rows, depth_y), left[-ch2:], shifts[-2 * ch2 : -ch2], right[-ch2:]]
    upward, corner = jnp.concatenate(upward, axis=0), left[:ch2]
    sums, upward, corner = lax.optimization_barrier((sums, upward, corner))
    part = exchange(sums.reshape(slabs, -1, sums.shape[1]), "gz").sum(0)
    part, upward, corner = lax.optimization_barrier((part, upward, corner))
    low, corner = shifted(upward, "gz", 1), shifted(corner, "gz", -1)
    part = exchange(copies(part, tiles), "xy").sum(0)
    part, low, corner = lax.optimization_barrier((part, low, corner))
    sums = exchange(copies(part, slabs), "gz").reshape(sums.shape)
    features, input_grad = last(
        place, low, mid, high, left, corner, right, shifts, w1, odd, even, inner_values, edge_values, w2, w4
    )
    scale = 1.0 / math.sqrt(slabs * depth_z * width * depth_y)
    first_grad, first_bias_grad, second_grad, second_bias_grad = unpack(sums, scale, channels, ch1, ch2)
    return (
        features[:, :, None, :],
        input_grad.reshape(channels, depth_z, 2, depth_y),
        first_grad,
        first_bias_grad,
        second_grad,
        second_bias_grad,
    )


def solution(mesh):
    return jax.shard_map(
        shards,
        mesh=mesh,
        in_specs=(
            P(None, "gz", None, "xy", None, None),
            P(),
            P(),
            P(),
            P(),
            P(None, "gz", "xy", None),
        ),
        out_specs=(P(None, "gz", "xy", None), P(None, "gz", "xy", None), P(), P(), P(), P()),
        check_vma=False,
    )
```
